128 devices in a mesh: gx: 8 (over y, core), gy: 16 (over z, x).
Axes of the slice: x: 4, y: 4, z: 4, core: 2. Of those that a mesh axis runs over, the one named last changes fastest.
Arguments:
- points: bfloat16 [131072, 64], P(('gx', 'gy')), may hold values from -25 to 25
- solution: float32 [131072, 32], P(('gx', 'gy')), may hold values from -6 to 6
- residual: float32 [131072, 32], P(('gx', 'gy')), may hold values from -36 to 36
- near_leaves: int32 [256, 4], P(('gx', 'gy')), may hold values from 0 to 255, as said below
- node_skeleton: int32 [128, 128], P(('gx', 'gy')), may hold values from 0 to 1023, as said below
- upper_skeleton: int32 [127, 128], replicated, may hold values from 0 to 255, as said below
- far_nodes: int32 [256, 16], P(('gx', 'gy')), may hold values from 0 to 254, as said below
Outputs:
- solution_next: float32 [131072, 32], P(('gx', 'gy'))
- residual_next: float32 [131072, 32], P(('gx', 'gy'))
- matvec_image: float32 [131072, 32], P(('gx', 'gy'))
The draws below stay inside these ranges and needn't reach their ends.
Inputs may be any that keep to these rules, and one draw needn't show every extreme that they name: `near_leaves`: leaves are numbered in point order, 2 to a device in the flat device order. A leaf's 4 near leaves are distinct and lie on other devices of its gx row; the near leaves named by one device's leaves are all distinct, at most 1 of them lie on any one other device, and exactly 1 on some. `node_skeleton`: each row holds 128 distinct positions among its device's 1024 points. `upper_skeleton`: row u holds 128 distinct positions among the 256 skeleton points of nodes 2u+1 and 2u+2, those of 2u+1 first. `far_nodes`: each row holds 16 distinct tree nodes.
All inputs are finite; a program needn't handle non-finite values.
Results may differ from the reference program's by a relative error of at most 0.0033.
Values may be sent and summed in bfloat16 or wider, within the bound.
A program may use at most 128 MiB of HBM per device.

```python
import math
import jax
import jax.numpy as jnp
from jax import lax

D = 64
NRHS = 32
LEAF = 512
RANK = 128
NEAR = 4
FAR = 16
LEAF_DEV = 2
CPD = 1024
NPTS = 131072
LEAVES = 256
NODES = 255
N_GY = 16
DEVICES = 128


def draw_points(key, part):
    order = jax.random.permutation(jax.random.fold_in(key, 13), D).astype(jnp.float32)
    heavy = 36.0 * D / 64.0
    floor_var = 0.25
    base = jnp.clip(jax.random.normal(jax.random.fold_in(key, 17), (NPTS, D), jnp.float32), -4.0, 4.0)
    spread = jnp.sqrt(heavy * jnp.exp(-0.5 * order) + floor_var)
    return (base * spread[None, :]).astype(jnp.bfloat16)


def draw_residual(key, part):
    rise = 1.0 + 2.0 * jnp.arange(NPTS, dtype=jnp.float32)[:, None] / NPTS
    base = jnp.clip(jax.random.normal(key, (NPTS, NRHS), jnp.float32), -6.0, 6.0)
    return base * rise


def draw_near_leaves(key, part):
    request_total = LEAF_DEV * NEAR
    peer_count = N_GY - 1

    def one_device(device_key, device_number):
        shuffled = jax.random.permutation(jax.random.fold_in(device_key, 1), request_total)
        column = device_number % N_GY
        row_number = device_number // N_GY
        folded = shuffled % peer_count
        offset = 1 + (folded + N_GY // 2 - 1) % peer_count
        owner_slot = (column + offset) % N_GY
        request_order = jnp.arange(request_total)
        earlier = (owner_slot[:, None] == owner_slot[None, :]) & (request_order[None, :] < request_order[:, None])
        slot_number = jnp.sum(earlier.astype(jnp.int32), axis=1)
        starts = jax.random.randint(jax.random.fold_in(device_key, 2), (N_GY,), 0, LEAF_DEV)
        local_leaf = (starts[owner_slot] + slot_number) % LEAF_DEV
        return ((row_number * N_GY + owner_slot) * LEAF_DEV + local_leaf).astype(jnp.int32)
    device_keys = jax.random.split(jax.random.fold_in(key, 11), DEVICES)
    lists = jax.vmap(one_device)(device_keys, jnp.arange(DEVICES))
    return lists.reshape(LEAVES, NEAR)


def draw_node_skeleton(key, part):
    stride = CPD // RANK
    jitter = jax.random.randint(jax.random.fold_in(key, 3), (DEVICES, RANK), 0, stride)
    return (jnp.arange(RANK)[None, :] * stride + jitter).astype(jnp.int32)


def draw_upper_skeleton(key, part):
    choose_bits = jax.random.randint(jax.random.fold_in(key, 5), (DEVICES - 1, RANK), 0, 2)
    return (2 * jnp.arange(RANK)[None, :] + choose_bits).astype(jnp.int32)


def draw_far_nodes(key, part):
    spacing = NODES // FAR
    starts = jax.random.randint(jax.random.fold_in(key, 1), (LEAVES, 1), 0, NODES)
    jitter = jax.random.randint(jax.random.fold_in(key, 2), (LEAVES, FAR), 0, spacing)
    return ((starts + jnp.arange(FAR)[None, :] * spacing + jitter) % NODES).astype(jnp.int32)


def shard_levels(own_key, shape, cuts, low, top_value):
    gain = 1.0
    for axis_at, shards_of in cuts:
        steps = jax.random.uniform(jax.random.fold_in(jax.random.fold_in(own_key, 6), axis_at), (shards_of,), jnp.float32, low / len(cuts), top_value / len(cuts))
        gain = gain * jnp.repeat(jnp.exp(steps), shape[axis_at] // shards_of).reshape((-1,) + (1,) * (len(shape) - 1 - axis_at))
    return gain


def bell_draw(stream_key, extent, scale, most, cuts=(), kind=jnp.bfloat16):
    values = scale * jax.random.normal(stream_key, extent, jnp.float32)
    if cuts:
        values = values * shard_levels(stream_key, extent, cuts, -0.22, 0.18)
    return jnp.clip(values, -most, most).astype(kind)


def setup_inputs(seed: int = 0) -> dict:
    streams_of = jax.random.split(jax.random.key(seed), 8)
    return {
        "points": draw_points(jax.random.fold_in(streams_of[7], 71), 0),
        "solution": bell_draw(streams_of[1], (NPTS, NRHS), 1.0, 6.0, ((0, 128),), jnp.float32),
        "residual": draw_residual(jax.random.fold_in(streams_of[7], 71), 0),
        "near_leaves": draw_near_leaves(jax.random.fold_in(streams_of[7], 71), 0),
        "node_skeleton": draw_node_skeleton(jax.random.fold_in(streams_of[7], 71), 0),
        "upper_skeleton": draw_upper_skeleton(jax.random.fold_in(streams_of[7], 71), 0),
        "far_nodes": draw_far_nodes(jax.random.fold_in(streams_of[7], 71), 0),
    }


LAMBDA_RIDGE = 1.0
FULL_PRECISION = lax.Precision.HIGHEST

def kernel_tile(left_points, right_points):
    left_square = lax.optimization_barrier(jnp.sum(jnp.square(left_points.astype(jnp.float32)), axis=-1))
    right_square = lax.optimization_barrier(jnp.sum(jnp.square(right_points.astype(jnp.float32)), axis=-1))
    cross_term = jnp.dot(left_points, right_points.T, preferred_element_type=jnp.float32)
    distance = left_square[:, None] + right_square[None, :] - 2.0 * cross_term
    return jnp.exp(distance * (-0.5 / left_points.shape[-1]))

def kernel_batch(left_points, right_points):
    left_wide = left_points.astype(jnp.float32)
    right_wide = right_points.astype(jnp.float32)
    left_square = lax.optimization_barrier(jnp.sum(left_wide * left_wide, axis=-1))
    right_square = lax.optimization_barrier(jnp.sum(right_wide * right_wide, axis=-1))
    cross_term = jnp.einsum('bmd,bnd->bmn', left_wide, right_wide, precision=FULL_PRECISION)
    distance = left_square[:, :, None] + right_square[:, None, :] - 2.0 * cross_term
    return jnp.exp(distance * (-0.5 / left_points.shape[-1]))

def far_kernel(own_points, far_points):
    own_wide = own_points.astype(jnp.float32)
    far_wide = far_points.astype(jnp.float32)
    own_square = lax.optimization_barrier(jnp.sum(own_wide * own_wide, axis=-1))
    far_square = lax.optimization_barrier(jnp.sum(far_wide * far_wide, axis=-1))
    cross_term = jnp.einsum('id,frd->fir', own_wide, far_wide, precision=FULL_PRECISION)
    distance = own_square[None, :, None] + far_square[:, None, :] - 2.0 * cross_term
    return jnp.exp(distance * (-0.5 / own_points.shape[-1]))

def cholesky_solve(matrix, right_side):
    order = matrix.shape[0]
    indices = jnp.arange(order, dtype=jnp.int32)

    def unit(column):
        return (indices == column).astype(matrix.dtype)

    def factor_step(column, lower):
        pick = unit(column)
        matrix_column = jnp.dot(matrix, pick, precision=FULL_PRECISION)
        lower_row = jnp.dot(pick, lower, precision=FULL_PRECISION)
        remainder = matrix_column - jnp.dot(lower, lower_row, precision=FULL_PRECISION)
        pivot = jnp.sqrt(jnp.sum(remainder * pick))
        new_column = jnp.where(indices >= column, remainder / pivot, jnp.zeros_like(remainder))
        return lower + new_column[:, None] * pick[None, :]
    lower = lax.fori_loop(0, order, factor_step, jnp.zeros_like(matrix))
    diagonal_part = lax.optimization_barrier(jnp.sum(lower * jnp.eye(order, dtype=matrix.dtype), axis=1))

    def forward_step(column, partial_value):
        pick = unit(column)
        lower_row = jnp.dot(pick, lower, precision=FULL_PRECISION)
        value = (jnp.dot(pick, right_side, precision=FULL_PRECISION) - jnp.dot(lower_row, partial_value, precision=FULL_PRECISION)) / jnp.sum(diagonal_part * pick)
        return partial_value + pick[:, None] * value[None, :]
    half_solve = lax.fori_loop(0, order, forward_step, jnp.zeros_like(right_side))

    def backward_step(count, partial_value):
        column = order - 1 - count
        pick = unit(column)
        lower_column = jnp.dot(lower, pick, precision=FULL_PRECISION)
        value = (jnp.dot(pick, half_solve, precision=FULL_PRECISION) - jnp.dot(lower_column, partial_value, precision=FULL_PRECISION)) / jnp.sum(diagonal_part * pick)
        return partial_value + pick[:, None] * value[None, :]
    return lax.fori_loop(0, order, backward_step, jnp.zeros_like(right_side))

def build_levels(level_points, level_weights, upper_skeleton, level_top, level_stop, block_index):
    point_levels = [level_points]
    weight_levels = [level_weights]
    for level_now in range(level_top - 1, level_stop - 1, -1):
        half_count = level_points.shape[0] // 2
        child_points = level_points.reshape(half_count, 2 * level_points.shape[1], level_points.shape[2])
        child_weights = level_weights.reshape(half_count, 2 * level_weights.shape[1], level_weights.shape[2])
        pick_rows = lax.dynamic_slice_in_dim(upper_skeleton, 2 ** level_now - 1 + block_index * half_count, half_count, 0)
        level_points = jax.vmap(lambda group_points, group_picks: jnp.take(group_points, group_picks, axis=0))(child_points, pick_rows)
        transfer = kernel_batch(level_points, child_points)
        level_weights = jnp.einsum('bmn,bnc->bmc', transfer, child_weights, precision=FULL_PRECISION) / lax.optimization_barrier(jnp.sum(transfer, axis=2))[:, :, None]
        point_levels.insert(0, level_points)
        weight_levels.insert(0, level_weights)
    return (point_levels, weight_levels)

def leaf_image(own_points, near_points, near_values, far_points, far_weights):
    near_tiles = jax.vmap(lambda other_points: kernel_tile(own_points, other_points))(near_points).astype(jnp.bfloat16)
    near_part = jnp.einsum('nij,njc->ic', near_tiles.astype(jnp.float32), near_values.astype(jnp.float32), precision=FULL_PRECISION)
    far_tiles = far_kernel(own_points, far_points)
    far_part = jnp.einsum('fir,frc->ic', far_tiles, far_weights, precision=FULL_PRECISION)
    return near_part / math.sqrt(own_points.shape[0]) + far_part / far_points.shape[1]

def reference(points, solution, residual, near_leaves, node_skeleton, upper_skeleton, far_nodes):
    values_half = residual.astype(jnp.bfloat16)
    leaf_points = points.reshape(LEAVES, LEAF, D)
    leaf_values = values_half.reshape(LEAVES, LEAF, NRHS)

    def device_node(inputs):
        device_points, device_residual, skeleton_row = inputs
        skeleton_points = jnp.take(device_points, skeleton_row, axis=0)
        kernel = kernel_tile(skeleton_points, device_points)
        return (skeleton_points, jnp.dot(kernel, device_residual, precision=FULL_PRECISION) / math.sqrt(CPD))
    node_points, node_weights = lax.map(device_node, (points.reshape(DEVICES, CPD, D), residual.reshape(DEVICES, CPD, NRHS), node_skeleton))
    depth_total = DEVICES.bit_length() - 1
    point_levels, weight_levels = build_levels(node_points, node_weights, upper_skeleton, depth_total, 0, 0)
    tree_points = jnp.concatenate(point_levels, axis=0)
    tree_weights = jnp.concatenate(weight_levels, axis=0)

    def one_leaf(inputs):
        leaf_number, near_row, far_row = inputs
        own_points = leaf_points[leaf_number]
        near_points = jnp.concatenate([own_points[None], jnp.take(leaf_points, near_row, axis=0)], axis=0)
        near_values = jnp.concatenate([leaf_values[leaf_number][None], jnp.take(leaf_values, near_row, axis=0)], axis=0)
        return leaf_image(own_points, near_points, near_values, jnp.take(tree_points, far_row, axis=0), jnp.take(tree_weights, far_row, axis=0))
    leaf_terms = lax.map(one_leaf, (jnp.arange(LEAVES, dtype=jnp.int32), near_leaves, far_nodes))
    matvec_image = LAMBDA_RIDGE * residual + leaf_terms.reshape(NPTS, NRHS)
    gram_matrix = jnp.dot(matvec_image.T, matvec_image, precision=FULL_PRECISION)
    cross_product = jnp.dot(matvec_image.T, residual, precision=FULL_PRECISION)
    step_coeffs = cholesky_solve(gram_matrix, cross_product)
    solution_next = solution + jnp.dot(residual, step_coeffs, precision=FULL_PRECISION)
    residual_next = residual - jnp.dot(matvec_image, step_coeffs, precision=FULL_PRECISION)
    return (solution_next, residual_next, matvec_image)
```

```python
import math

import jax
import jax.numpy as jnp
from jax import lax
from jax.experimental import pallas as pl
from jax.experimental.pallas import tpu as pltpu
from jax.sharding import PartitionSpec as P

D = 64
NRHS = 32
LEAF = 512
RANK = 128
NEAR = 4
FAR = 16
CPD = 1024
N_GX = 8
N_GY = 16
N_Y = 4
NODES = 255
FIRST = 127
AUG = D + 16
PAY = AUG + NRHS
REQ = PAY + 16
LEAF_ROWS = D + NRHS
SCALE = math.log2(math.e) / D
FULL = lax.Precision.HIGHEST
F32, BF16 = jnp.float32, jnp.bfloat16
MESH = pl.DeviceIdType.MESH


def dot(a, b, contract=((1,), (0,)), precision=None):
    return lax.dot_general(a, b, (contract, ((), ())), precision=precision, preferred_element_type=F32)


def square_rows(wide):
    half = -0.5 * jnp.sum(wide * wide, axis=0, keepdims=True)
    high = half.astype(BF16).astype(F32)
    rest = half - high
    middle = rest.astype(BF16).astype(F32)
    low = rest - middle
    row = lax.broadcasted_iota(jnp.int32, (16, wide.shape[1]), 0)
    ones = jnp.where((row >= 4) & (row < 7), 1.0, 0.0)
    return jnp.where(row == 0, high, jnp.where(row == 1, middle, jnp.where(row == 2, low, ones)))


def turned(rows):
    return jnp.concatenate([pltpu.roll(rows[:8], 4, 0), rows[8:]], axis=0)


def kernel_body(
    points, residual, near, requests, skeleton, upper, far,
    image, coeffs,
    nodes, own, own_right, own_left, stage, near_in, near_acc, far_acc, part1, part2,
    pay_s, pay_r, near_s, near_r, y_s, y_r, sib_s, sib_r, one_s, one_r, two_s, two_r,
):
    gx, gy = lax.axis_index("gx"), lax.axis_index("gy")
    y, core = gx // 2, gx % 2
    me = gx * N_GY + gy
    sibling = 2 * y + (1 - core)

    barrier = pltpu.get_barrier_semaphore()

    @pl.loop(1, N_GY)
    def _(k):
        pl.semaphore_signal(barrier, inc=1, device_id=(gx, (gy + k) % N_GY), device_id_type=MESH)

    @pl.loop(1, N_GX)
    def _(k):
        pl.semaphore_signal(barrier, inc=1, device_id=((gx + k) % N_GX, gy), device_id_type=MESH)

    for leaf in range(2):
        at = pl.ds(leaf * LEAF, LEAF)
        wide = points[:, at].astype(F32)
        rows = square_rows(wide)
        own_right[leaf, 0:D] = points[:, at]
        own_right[leaf, D:AUG] = rows.astype(BF16)
        both = jnp.concatenate([wide, turned(rows), jnp.zeros((48, LEAF), F32)], axis=0)
        own_left[leaf] = both.T.astype(BF16)
        own[leaf, 0:D] = points[:, at]
        own[leaf, D:LEAF_ROWS] = residual[:, at].astype(BF16)
    pick = skeleton[...]
    skel = jnp.zeros((D, RANK), F32)
    for leaf in range(2):
        place = lax.broadcasted_iota(jnp.int32, (LEAF, RANK), 0) + leaf * LEAF
        skel += dot(points[:, pl.ds(leaf * LEAF, LEAF)], jnp.where(place == pick, 1.0, 0.0).astype(BF16))
    rows = square_rows(skel)
    left = jnp.concatenate([skel, turned(rows), jnp.zeros((48, RANK), F32)], axis=0).T.astype(BF16)
    weights = jnp.zeros((NRHS, RANK), F32)
    for leaf in range(2):
        tile = jnp.exp2(SCALE * dot(left[:, :AUG], own_right[leaf]))
        weights += dot(residual[:, pl.ds(leaf * LEAF, LEAF)], tile, ((1,), (1,)), FULL)
    mine = FIRST + me
    nodes[mine, 0:D] = skel.astype(BF16)
    nodes[mine, D:AUG] = rows.astype(BF16)
    nodes[mine, AUG:PAY] = (weights * (1.0 / math.sqrt(CPD))).astype(BF16)
    nodes[mine, PAY:REQ] = requests[...]

    pl.semaphore_wait(barrier, N_GY - 1 + N_GX - 1)

    def pay_copy(k, slot):
        peer = (gy + k) % N_GY
        return pltpu.make_async_remote_copy(
            src_ref=nodes.at[mine], dst_ref=nodes.at[slot],
            send_sem=pay_s.at[peer], recv_sem=pay_r.at[slot - FIRST - gx * N_GY],
            device_id=(gx, peer), device_id_type=MESH,
        )

    @pl.loop(1, N_GY)
    def _(k):
        pay_copy(k, mine).start()

    def tiles(leaf, right, values, acc, first):
        for c in range(4):
            at = pl.ds(c * 128, 128)
            tile = jnp.exp2(SCALE * dot(own_left[leaf, at, :AUG], right)).astype(BF16)
            term = dot(values, tile, ((1,), (1,)))
            acc[leaf, :, at] = term if first else acc[leaf, :, at] + term

    for leaf in range(2):
        tiles(leaf, own_right[leaf], own[leaf, D:LEAF_ROWS], near_acc, True)

    asked = (2 * me + 1).astype(F32)
    near_in[gy] = own[0]

    def near_copy(peer, slot):
        return pltpu.make_async_remote_copy(
            src_ref=stage.at[peer], dst_ref=near_in.at[slot],
            send_sem=near_s.at[peer], recv_sem=near_r.at[slot],
            device_id=(gx, peer), device_id_type=MESH,
        )

    @pl.loop(1, N_GY)
    def _(k):
        peer = (gy + k) % N_GY
        slot = FIRST + gx * N_GY + peer
        pay_copy(k, slot).wait_recv()
        want = nodes[slot, PAY:REQ].astype(F32)
        second = jnp.max(jnp.where(want == asked, 1.0, 0.0), axis=0, keepdims=True)
        second = jnp.concatenate([second] * 4, axis=1)
        for r in range(0, LEAF_ROWS, 32):
            at = pl.ds(r, 32)
            pick_second = jnp.broadcast_to(second, (32, LEAF))
            stage[peer, at] = jnp.where(
                pick_second > 0.5, own[1, at].astype(F32), own[0, at].astype(F32)
            ).astype(BF16)
        near_copy(peer, gy).start()

    def block(row):
        return nodes.at[pl.ds(FIRST + row * N_GY, N_GY), pl.ds(0, PAY)]

    def y_copy(k, row):
        other = (y + k) % N_Y
        return pltpu.make_async_remote_copy(
            src_ref=block(gx), dst_ref=block(row),
            send_sem=y_s.at[other], recv_sem=y_r.at[row // 2],
            device_id=(2 * other + core, gy), device_id_type=MESH,
        )

    def sib_copy(other, row):
        return pltpu.make_async_remote_copy(
            src_ref=block(2 * other + core), dst_ref=block(row),
            send_sem=sib_s.at[other], recv_sem=sib_r.at[row // 2],
            device_id=(sibling, gy), device_id_type=MESH,
        )

    for k in (1, 3, 2):
        y_copy(k, gx).start()
    sib_copy(y, gx).start()

    place = lax.broadcasted_iota(jnp.int32, (2 * RANK, RANK), 0)

    def build(first, count):
        done = []
        for i in range(count):
            u = first + i
            a, b = nodes[2 * u + 1, 0:PAY], nodes[2 * u + 2, 0:PAY]
            choice = jnp.where(place == upper[pl.ds(u, 1), :], 1.0, 0.0).astype(BF16)
            right = dot(jnp.concatenate([a[:AUG], b[:AUG]], axis=1), choice)
            left = jnp.concatenate([right[:D], turned(right[D:])], axis=0).astype(BF16)
            both = jnp.concatenate([a[:AUG], b[:AUG]], axis=1)
            tile = jnp.exp2(SCALE * dot(both, left, ((0,), (0,)))).astype(BF16)
            sums = dot(jnp.concatenate([a[D:], b[D:]], axis=1), tile)
            done.append((right.astype(BF16), (sums[16:] / sums[4:5]).astype(BF16)))
        for i, (right, weights) in enumerate(done):
            nodes[first + i, 0:AUG] = right
            nodes[first + i, AUG:PAY] = weights

    def build_row(row):
        build(63 + row * 8, 4)
        build(67 + row * 8, 4)
        build(31 + row * 4, 4)
        build(15 + row * 2, 2)
        build(7 + row, 1)

    build_row(gx)
    sib_copy(y, sibling).wait_recv()
    build_row(sibling)

    @pl.loop(1, N_Y)
    def _(k):
        other = (y + k) % N_Y
        y_copy(k, 2 * other + core).wait_recv()
        sib_copy(other, 2 * other + core).start()
        build_row(2 * other + core)

    @pl.loop(1, N_GY)
    def _(k):
        peer = (gy + k) % N_GY
        near_copy(peer, peer).wait_recv()

    for leaf in range(2):

        @pl.loop(0, NEAR)
        def _(n, leaf=leaf):
            got = near_in[(near[leaf, n] // 2) % N_GY]
            right = jnp.concatenate([got[:D], square_rows(got[:D].astype(F32)).astype(BF16)], axis=0)
            tiles(leaf, right, got[D:], near_acc, False)

    @pl.loop(1, N_Y)
    def _(k):
        other = (y + k) % N_Y
        row = 2 * other + 1 - core
        sib_copy(other, row).wait_recv()
        build_row(row)

    build(3, 4)
    build(1, 2)
    build(0, 1)

    far_acc[...] = jnp.zeros_like(far_acc)
    for leaf in range(2):

        @pl.loop(0, FAR // 4)
        def _(n, leaf=leaf):
            got = jnp.concatenate([nodes[far[leaf, 4 * n + i], 0:PAY] for i in range(4)], axis=1)
            tiles(leaf, got[:AUG], got[AUG:], far_acc, False)

    for leaf in range(2):
        at = pl.ds(leaf * LEAF, LEAF)
        image[:, at] = (
            residual[:, at] + near_acc[leaf] * (1.0 / math.sqrt(LEAF)) + far_acc[leaf] * (1.0 / RANK)
        )

    both = jnp.concatenate([image[...], residual[...]], axis=0)
    gram = dot(image[...], both, ((1,), (1,)), FULL)
    part1[gy] = jnp.concatenate([gram[:16], gram[16:]], axis=1)

    def one_copy(peer, slot):
        return pltpu.make_async_remote_copy(
            src_ref=part1.at[gy], dst_ref=part1.at[slot],
            send_sem=one_s.at[peer], recv_sem=one_r.at[slot],
            device_id=(gx, peer), device_id_type=MESH,
        )

    def two_copy(peer, slot):
        return pltpu.make_async_remote_copy(
            src_ref=part2.at[gx], dst_ref=part2.at[slot],
            send_sem=two_s.at[peer], recv_sem=two_r.at[slot],
            device_id=(peer, gy), device_id_type=MESH,
        )

    @pl.loop(1, N_GY)
    def _(k):
        one_copy((gy + k) % N_GY, gy).start()

    @pl.loop(1, N_GY)
    def _(k):
        peer = (gy + k) % N_GY
        one_copy(peer, peer).wait_recv()

    total = part1[0]
    for k in range(1, N_GY):
        total += part1[k]
    part2[gx] = total

    @pl.loop(1, N_GX)
    def _(k):
        two_copy((gx + k) % N_GX, gx).start()

    @pl.loop(1, N_GX)
    def _(k):
        peer = (gx + k) % N_GX
        two_copy(peer, peer).wait_recv()

    total = part2[0]
    for k in range(1, N_GX):
        total += part2[k]

    work = jnp.concatenate([total, pltpu.roll(total, 64, 1)], axis=0)
    row = lax.broadcasted_iota(jnp.int32, (NRHS, 128), 0)
    for k in range(NRHS):
        pivot_row = work[k : k + 1] / work[k : k + 1, k : k + 1]
        work = jnp.where(row == k, pivot_row, work - work[:, k : k + 1] * pivot_row)
    coeffs[...] = work

    @pl.loop(1, N_GY)
    def _(k):
        peer = (gy + k) % N_GY
        pay_copy(k, mine).wait_send()
        near_copy(peer, gy).wait_send()
        one_copy(peer, gy).wait_send()

    @pl.loop(1, N_GX)
    def _(k):
        two_copy((gx + k) % N_GX, gx).wait_send()

    for k in (1, 3, 2):
        y_copy(k, gx).wait_send()

    @pl.loop(0, N_Y)
    def _(k):
        sib_copy((y + k) % N_Y, gx).wait_send()


def shards(points, solution, residual, near_leaves, node_skeleton, upper_skeleton, far_nodes):
    requests = jnp.concatenate([near_leaves.reshape(-1), jnp.full((8,), -1, jnp.int32)])
    requests = jnp.broadcast_to(requests.astype(BF16)[:, None], (16, 128))
    vmem, smem = (pl.BlockSpec(memory_space=m) for m in (pltpu.VMEM, pltpu.SMEM))
    dma = pltpu.SemaphoreType.DMA
    residual_t = residual.T
    image_t, work = pl.pallas_call(
        kernel_body,
        out_shape=(
            jax.ShapeDtypeStruct((NRHS, CPD), F32),
            jax.ShapeDtypeStruct((NRHS, 128), F32),
        ),
        in_specs=[vmem, vmem, smem, vmem, vmem, vmem, smem],
        out_specs=(vmem, vmem),
        scratch_shapes=[
            pltpu.VMEM((NODES, REQ, RANK), BF16),
            pltpu.VMEM((2, LEAF_ROWS, LEAF), BF16),
            pltpu.VMEM((2, AUG, LEAF), BF16),
            pltpu.VMEM((2, LEAF, 128), BF16),
            pltpu.VMEM((N_GY, LEAF_ROWS, LEAF), BF16),
            pltpu.VMEM((N_GY, LEAF_ROWS, LEAF), BF16),
            pltpu.VMEM((2, NRHS, LEAF), F32),
            pltpu.VMEM((2, NRHS, LEAF), F32),
            pltpu.VMEM((N_GY, 16, 128), F32),
            pltpu.VMEM((N_GX, 16, 128), F32),
            dma((N_GY,)), dma((N_GY,)), dma((N_GY,)), dma((N_GY,)),
            dma((N_Y,)), dma((N_Y,)), dma((N_Y,)), dma((N_Y,)),
            dma((N_GY,)), dma((N_GY,)), dma((N_GX,)), dma((N_GX,)),
        ],
        compiler_params=pltpu.CompilerParams(
            collective_id=0, has_side_effects=True, vmem_limit_bytes=48 * 2**20
        ),
    )(points.T, residual_t, near_leaves, requests, node_skeleton, upper_skeleton, far_nodes)
    step = work[:, NRHS : 2 * NRHS]
    solution_next = solution.T + dot(step, residual_t, ((0,), (0,)), FULL)
    residual_next = residual_t - dot(step, image_t, ((0,), (0,)), FULL)
    return solution_next.T, residual_next.T, image_t.T


def solution(mesh):
    split = P(("gx", "gy"), None)
    return jax.shard_map(
        shards,
        mesh=mesh,
        in_specs=(split, split, split, split, split, P(), split),
        out_specs=(split, split, split),
        check_vma=False,
    )
```

```python
import math

import jax
import jax.numpy as jnp
from jax import lax
from jax.experimental import pallas as pl
from jax.experimental.pallas import tpu as pltpu
from jax.sharding import PartitionSpec as P

D = 64
NRHS = 32
LEAF = 512
RANK = 128
NEAR = 4
FAR = 16
CPD = 1024
N_GX = 8
N_GY = 16
N_Y = 4
NODES = 255
FIRST = 127
AUG = D + 16
PAY = AUG + NRHS
LEAF_ROWS = D + NRHS
SCALE = math.log2(math.e) / D
FULL = lax.Precision.HIGHEST
F32, BF16 = jnp.float32, jnp.bfloat16
MESH = pl.DeviceIdType.MESH


def dot(a, b, contract=((1,), (0,)), precision=None):
    return lax.dot_general(a, b, (contract, ((), ())), precision=precision, preferred_element_type=F32)


def square_rows(wide):
    half = -0.5 * jnp.sum(wide * wide, axis=0, keepdims=True)
    high = half.astype(BF16).astype(F32)
    rest = half - high
    middle = rest.astype(BF16).astype(F32)
    low = rest - middle
    row = lax.broadcasted_iota(jnp.int32, (16, wide.shape[1]), 0)
    ones = jnp.where((row >= 4) & (row < 7), 1.0, 0.0)
    return jnp.where(row == 0, high, jnp.where(row == 1, middle, jnp.where(row == 2, low, ones)))


def turned(rows):
    return jnp.concatenate([pltpu.roll(rows[:8], 4, 0), rows[8:]], axis=0)


def kernel_body(
    points_in, residual_in, near_in, skeleton_in, upper_in, far_in,
    image, coeffs,
    points, residual, near, skeleton, upper, far,
    nodes, own, own_right, own_left, asked, stage, leaves, near_acc, far_acc, part1, part2,
    in_s, req_s, req_r, pay_s, pay_r, near_s, near_r, y_s, y_r, on_s, on_r, sib_s, sib_r,
    one_s, one_r, two_s, two_r,
):
    gx, gy = lax.axis_index("gx"), lax.axis_index("gy")
    y, core = gx // 2, gx % 2
    me = gx * N_GY + gy
    sibling = 2 * y + (1 - core)

    pairs = ((near_in, near), (skeleton_in, skeleton), (points_in, points), (residual_in, residual), (upper_in, upper), (far_in, far))
    loads = [pltpu.make_async_copy(a, b, in_s.at[i]) for i, (a, b) in enumerate(pairs)]
    for load in loads:
        load.start()

    barrier = pltpu.get_barrier_semaphore()

    @pl.loop(1, N_GY)
    def _(k):
        pl.semaphore_signal(barrier, inc=1, device_id=(gx, (gy + k) % N_GY), device_id_type=MESH)

    @pl.loop(1, N_GX)
    def _(k):
        pl.semaphore_signal(barrier, inc=1, device_id=((gx + k) % N_GX, gy), device_id_type=MESH)

    def copy(src, dst, send, recv, device):
        return pltpu.make_async_remote_copy(
            src_ref=src, dst_ref=dst, send_sem=send, recv_sem=recv, device_id=device, device_id_type=MESH
        )

    loads[0].wait()
    row = lax.broadcasted_iota(jnp.int32, (16, 128), 0)
    wanted = jnp.full((16, 128), -1, jnp.int32)
    for leaf in range(2):
        for n in range(NEAR):
            wanted = jnp.where(row == leaf * NEAR + n, near[leaf, n], wanted)
    asked[gy] = wanted.astype(F32).astype(BF16)
    for load in loads[1:]:
        load.wait()

    for leaf in range(2):
        at = pl.ds(leaf * LEAF, LEAF)
        wide = points[:, at].astype(F32)
        rows = square_rows(wide)
        own_right[leaf, 0:D] = points[:, at]
        own_right[leaf, D:AUG] = rows.astype(BF16)
        both = jnp.concatenate([wide, turned(rows), jnp.zeros((48, LEAF), F32)], axis=0)
        own_left[leaf] = both.T.astype(BF16)
        own[leaf, 0:D] = points[:, at]
        own[leaf, D:LEAF_ROWS] = residual[:, at].astype(BF16)
    pick = skeleton[...]
    skel = jnp.zeros((D, RANK), F32)
    for leaf in range(2):
        place = lax.broadcasted_iota(jnp.int32, (LEAF, RANK), 0) + leaf * LEAF
        skel += dot(points[:, pl.ds(leaf * LEAF, LEAF)], jnp.where(place == pick, 1.0, 0.0).astype(BF16))
    rows = square_rows(skel)
    left = jnp.concatenate([skel, turned(rows), jnp.zeros((48, RANK), F32)], axis=0).T.astype(BF16)
    weights = jnp.zeros((NRHS, RANK), F32)
    for leaf in range(2):
        tile = jnp.exp2(SCALE * dot(left[:, :AUG], own_right[leaf]))
        weights += dot(residual[:, pl.ds(leaf * LEAF, LEAF)], tile, ((1,), (1,)), FULL)
    mine = FIRST + me
    nodes[mine, 0:D] = skel.astype(BF16)
    nodes[mine, D:AUG] = rows.astype(BF16)
    nodes[mine, AUG:PAY] = (weights * (1.0 / math.sqrt(CPD))).astype(BF16)

    pl.semaphore_wait(barrier, N_GY - 1 + N_GX - 1)

    def req_copy(peer, slot):
        return copy(asked.at[gy], asked.at[slot], req_s.at[peer], req_r.at[slot], (gx, peer))

    def pay_copy(peer, slot):
        at = FIRST + gx * N_GY + slot
        return copy(nodes.at[mine], nodes.at[at], pay_s.at[peer], pay_r.at[slot], (gx, peer))

    def near_copy(peer, slot):
        return copy(stage.at[peer], leaves.at[slot], near_s.at[peer], near_r.at[slot], (gx, peer))

    @pl.loop(1, N_GY)
    def _(k):
        req_copy((gy + k) % N_GY, gy).start()

    @pl.loop(1, N_GY)
    def _(k):
        pay_copy((gy + k) % N_GY, gy).start()

    this = (2 * me + 1).astype(F32)
    leaves[gy] = own[0]

    @pl.loop(1, N_GY)
    def _(k):
        peer = (gy + k) % N_GY
        req_copy(peer, peer).wait_recv()
        second = jnp.where(asked[peer].astype(F32) == this, 1.0, 0.0)
        second = jnp.max(second, axis=0, keepdims=True)
        second = jnp.concatenate([second] * 4, axis=1)
        for r in range(0, LEAF_ROWS, 32):
            at = pl.ds(r, 32)
            stage[peer, at] = jnp.where(
                jnp.broadcast_to(second, (32, LEAF)) > 0.5, own[1, at].astype(F32), own[0, at].astype(F32)
            ).astype(BF16)
        near_copy(peer, gy).start()

    def tile_term(leaf, right, values):
        tile = jnp.exp2(SCALE * dot(own_left[leaf, :, :AUG], right)).astype(BF16)
        return dot(tile, values, ((1,), (1,)))

    @pl.loop(0, 2)
    def _(leaf):
        near_acc[leaf] = tile_term(leaf, own_right[leaf], own[leaf, D:LEAF_ROWS])

    @pl.loop(1, N_GY)
    def _(k):
        peer = (gy + k) % N_GY
        pay_copy(peer, peer).wait_recv()

    def half(row, h):
        return nodes.at[pl.ds(FIRST + row * N_GY + h * 8, 8)]

    def row_of(step, other=False):
        return 2 * ((y + step) % N_Y) + (1 - core if other else core)

    def y_copy(step, h, source):
        to = (row_of(step), gy)
        k = 0 if step == 1 else 1
        return copy(half(gx, h), half(row_of(source), h), y_s.at[k, h], y_r.at[k, h], to)

    def on_copy(step, source):
        h = k = 0 if step == 1 else 1
        return copy(half(row_of(-step), h), half(row_of(source), h), on_s.at[k], on_r.at[k], (row_of(step), gy))

    def sib_copy(step, h, other):
        at = (y + step) % N_Y
        return copy(half(row_of(step), h), half(row_of(step, other), h), sib_s.at[at, h], sib_r.at[at, h], (sibling, gy))

    for h in range(2):
        y_copy(1, h, 0).start()
        y_copy(-1, 1 - h, 0).start()
    for h in range(2):
        sib_copy(0, h, False).start()

    def build(first, count):
        done = []
        for i in range(count):
            u = first + i
            a, b = nodes[2 * u + 1], nodes[2 * u + 2]
            choice = jnp.broadcast_to(upper[pl.ds(u, 1), :], (AUG, RANK))
            lane = jnp.bitwise_and(choice, RANK - 1)
            from_a, from_b = (
                jnp.take_along_axis(x[:AUG].astype(F32), lane, axis=1, mode="promise_in_bounds") for x in (a, b)
            )
            right = jnp.where(choice < RANK, from_a, from_b)
            left = jnp.concatenate([right[:D], turned(right[D:])], axis=0).astype(BF16)
            both = jnp.concatenate([a, b], axis=1)
            tile = jnp.exp2(SCALE * dot(left, both[:AUG], ((0,), (0,)))).astype(BF16)
            sums = dot(both[D:], tile, ((1,), (1,)))
            done.append((right.astype(BF16), (sums[16:] / sums[4:5]).astype(BF16)))
        for i, (right, weights) in enumerate(done):
            nodes[first + i, 0:AUG] = right
            nodes[first + i, AUG:PAY] = weights

    def build_row(row):
        build(63 + row * 8, 8)
        build(31 + row * 4, 4)
        build(15 + row * 2, 2)
        build(7 + row, 1)

    def near_tile(n):
        leaf = n // NEAR
        got = leaves[(near[leaf, n % NEAR] // 2) % N_GY]
        right = jnp.concatenate([got[:D], square_rows(got[:D].astype(F32)).astype(BF16)], axis=0)
        near_acc[leaf] = near_acc[leaf] + tile_term(leaf, right, got[D:])

    @pl.loop(0, N_GX)
    def _(i):
        @pl.when(i == 1)
        def _():
            for step in (1, -1):
                h = 0 if step == 1 else 1
                y_copy(step, h, -step).wait_recv()
                on_copy(step, -step).start()
                sib_copy(-step, h, False).start()
            for h in range(2):
                sib_copy(0, h, True).wait_recv()

        @pl.when(i == 2)
        def _():
            for step in (-1, 1):
                h = 1 if step == 1 else 0
                y_copy(step, h, -step).wait_recv()
                sib_copy(-step, h, False).start()

        @pl.when(i == 3)
        def _():
            for h in range(2):
                sib_copy(1, h, True).wait_recv()

        @pl.when(i == 5)
        def _():
            for h in range(2):
                sib_copy(-1, h, True).wait_recv()

        @pl.when(i == 6)
        def _():
            for step in (1, -1):
                on_copy(step, 2).wait_recv()
                sib_copy(2, 0 if step == 1 else 1, False).start()

        @pl.when(i == 7)
        def _():
            @pl.loop(1, N_GY)
            def _(k):
                peer = (gy + k) % N_GY
                near_copy(peer, peer).wait_recv()

            pl.loop(0, 2 * NEAR)(near_tile)
            for h in range(2):
                sib_copy(2, h, True).wait_recv()

        turn = i // 2
        away = turn + turn // 2 - 2 * (turn // 3)
        build_row(2 * ((y + away) % N_Y) + (core + i % 2) % 2)

    build(3, 4)
    build(1, 2)
    build(0, 1)

    far_acc[...] = jnp.zeros_like(far_acc)

    @pl.loop(0, FAR // 2)
    def _(n):
        leaf, group = n // (FAR // 4), n % (FAR // 4)
        got = jnp.concatenate([nodes[far[leaf, 4 * group + i]] for i in range(4)], axis=1)
        far_acc[leaf] = far_acc[leaf] + tile_term(leaf, got[:AUG], got[AUG:])

    for leaf in range(2):
        at = pl.ds(leaf * LEAF, LEAF)
        terms = near_acc[leaf] * (1.0 / math.sqrt(LEAF)) + far_acc[leaf] * (1.0 / RANK)
        image[:, at] = residual[:, at] + terms.T

    both = jnp.concatenate([image[...], residual[...]], axis=0)
    gram = dot(image[...], both, ((1,), (1,)), FULL)
    part1[gy] = jnp.concatenate([gram[:16], gram[16:]], axis=1)

    def one_copy(peer, slot):
        return copy(part1.at[gy], part1.at[slot], one_s.at[peer], one_r.at[slot], (gx, peer))

    def two_copy(peer, slot):
        return copy(part2.at[gx], part2.at[slot], two_s.at[peer], two_r.at[slot], (peer, gy))

    @pl.loop(1, N_GY)
    def _(k):
        one_copy((gy + k) % N_GY, gy).start()

    @pl.loop(1, N_GY)
    def _(k):
        peer = (gy + k) % N_GY
        one_copy(peer, peer).wait_recv()

    total = part1[0]
    for k in range(1, N_GY):
        total += part1[k]
    part2[gx] = total

    @pl.loop(1, N_GX)
    def _(k):
        two_copy((gx + k) % N_GX, gx).start()

    @pl.loop(1, N_GX)
    def _(k):
        peer = (gx + k) % N_GX
        two_copy(peer, peer).wait_recv()

    total = part2[0]
    for k in range(1, N_GX):
        total += part2[k]

    work = jnp.concatenate([total, pltpu.roll(total, 64, 1)], axis=0)
    row = lax.broadcasted_iota(jnp.int32, (NRHS, 128), 0)
    for k in range(NRHS):
        pivot_row = work[k : k + 1] / work[k : k + 1, k : k + 1]
        work = jnp.where(row == k, pivot_row, work - work[:, k : k + 1] * pivot_row)
    coeffs[...] = work

    @pl.loop(1, N_GY)
    def _(k):
        peer = (gy + k) % N_GY
        req_copy(peer, gy).wait_send()
        pay_copy(peer, gy).wait_send()
        near_copy(peer, gy).wait_send()
        one_copy(peer, gy).wait_send()

    @pl.loop(1, N_GX)
    def _(k):
        two_copy((gx + k) % N_GX, gx).wait_send()

    for step in (1, -1):
        for h in range(2):
            y_copy(step, h, 0).wait_send()
        on_copy(step, -step).wait_send()
    for step in range(N_Y):
        for h in range(2):
            sib_copy(step, h, False).wait_send()


def shards(points, solution, residual, near_leaves, node_skeleton, upper_skeleton, far_nodes):
    vmem, hbm = (pl.BlockSpec(memory_space=m) for m in (pltpu.VMEM, pltpu.HBM))
    dma = pltpu.SemaphoreType.DMA
    residual_t = residual.T
    image_t, work = pl.pallas_call(
        kernel_body,
        out_shape=(
            jax.ShapeDtypeStruct((NRHS, CPD), F32),
            jax.ShapeDtypeStruct((NRHS, 128), F32),
        ),
        in_specs=[hbm] * 6,
        out_specs=(vmem, vmem),
        scratch_shapes=[
            pltpu.VMEM((D, CPD), BF16),
            pltpu.VMEM((NRHS, CPD), F32),
            pltpu.SMEM((2, NEAR), jnp.int32),
            pltpu.VMEM((1, RANK), jnp.int32),
            pltpu.VMEM((FIRST, RANK), jnp.int32),
            pltpu.SMEM((2, FAR), jnp.int32),
            pltpu.VMEM((NODES, PAY, RANK), BF16),
            pltpu.VMEM((2, LEAF_ROWS, LEAF), BF16),
            pltpu.VMEM((2, AUG, LEAF), BF16),
            pltpu.VMEM((2, LEAF, 128), BF16),
            pltpu.VMEM((N_GY, 16, 128), BF16),
            pltpu.VMEM((N_GY, LEAF_ROWS, LEAF), BF16),
            pltpu.VMEM((N_GY, LEAF_ROWS, LEAF), BF16),
            pltpu.VMEM((2, LEAF, NRHS), F32),
            pltpu.VMEM((2, LEAF, NRHS), F32),
            pltpu.VMEM((N_GY, 16, 128), F32),
            pltpu.VMEM((N_GX, 16, 128), F32),
            dma((6,)),
            dma((N_GY,)), dma((N_GY,)), dma((N_GY,)), dma((N_GY,)), dma((N_GY,)), dma((N_GY,)),
            dma((2, 2)), dma((2, 2)), dma((2,)), dma((2,)), dma((N_Y, 2)), dma((N_Y, 2)),
            dma((N_GY,)), dma((N_GY,)), dma((N_GX,)), dma((N_GX,)),
        ],
        compiler_params=pltpu.CompilerParams(
            collective_id=0, has_side_effects=True, vmem_limit_bytes=48 * 2**20
        ),
    )(points.T, residual_t, near_leaves, node_skeleton, upper_skeleton, far_nodes)
    step = work[:, NRHS : 2 * NRHS]
    solution_next = solution.T + dot(step, residual_t, ((0,), (0,)), FULL)
    residual_next = residual_t - dot(step, image_t, ((0,), (0,)), FULL)
    return solution_next.T, residual_next.T, image_t.T


def solution(mesh):
    split = P(("gx", "gy"), None)
    return jax.shard_map(
        shards,
        mesh=mesh,
        in_specs=(split, split, split, split, split, P(), split),
        out_specs=(split, split, split),
        check_vma=False,
    )
```

```python
import math

import jax
import jax.numpy as jnp
from jax import lax
from jax.experimental import pallas as pl
from jax.experimental.pallas import tpu as pltpu
from jax.sharding import PartitionSpec as P

D = 64
NRHS = 32
LEAF = 512
RANK = 128
NEAR = 4
FAR = 16
CPD = 1024
N_GX = 8
N_GY = 16
N_Y = 4
NODES = 255
FIRST = 127
AUG = D + 16
PAY = AUG + NRHS
LEAF_ROWS = D + NRHS
SCALE = math.log2(math.e) / D
FULL = lax.Precision.HIGHEST
F32, BF16 = jnp.float32, jnp.bfloat16
MESH = pl.DeviceIdType.MESH


def dot(a, b, contract=((1,), (0,)), precision=None):
    return lax.dot_general(a, b, (contract, ((), ())), precision=precision, preferred_element_type=F32)


def square_rows(wide):
    half = -0.5 * jnp.sum(wide * wide, axis=0, keepdims=True)
    high = half.astype(BF16).astype(F32)
    rest = half - high
    middle = rest.astype(BF16).astype(F32)
    low = rest - middle
    row = lax.broadcasted_iota(jnp.int32, (16, wide.shape[1]), 0)
    ones = jnp.where((row >= 4) & (row < 7), 1.0, 0.0)
    return jnp.where(row == 0, high, jnp.where(row == 1, middle, jnp.where(row == 2, low, ones)))


def turned(rows):
    return jnp.concatenate([pltpu.roll(rows[:8], 4, 0), rows[8:]], axis=0)


def kernel_body(
    points_in, residual_in, near_in, skeleton_in, upper_in, far_in,
    image, coeffs,
    points, residual, near, skeleton, upper, far,
    nodes, own, own_right, own_left, asked, stage, leaves, near_acc, far_acc, part1, part2,
    in_s, req_s, req_r, pay_s, pay_r, near_s, near_r, y_s, y_r, on_s, on_r, sib_s, sib_r,
    one_s, one_r, two_s, two_r,
):
    gx, gy = lax.axis_index("gx"), lax.axis_index("gy")
    y, core = gx // 2, gx % 2
    me = gx * N_GY + gy
    sibling = 2 * y + (1 - core)

    pairs = ((near_in, near), (skeleton_in, skeleton), (points_in, points), (residual_in, residual), (upper_in, upper), (far_in, far))
    loads = [pltpu.make_async_copy(a, b, in_s.at[i]) for i, (a, b) in enumerate(pairs)]
    for load in loads:
        load.start()

    barrier = pltpu.get_barrier_semaphore()

    @pl.loop(1, N_GY)
    def _(k):
        pl.semaphore_signal(barrier, inc=1, device_id=(gx, (gy + k) % N_GY), device_id_type=MESH)

    @pl.loop(1, N_GX)
    def _(k):
        pl.semaphore_signal(barrier, inc=1, device_id=((gx + k) % N_GX, gy), device_id_type=MESH)

    def copy(src, dst, send, recv, device):
        return pltpu.make_async_remote_copy(
            src_ref=src, dst_ref=dst, send_sem=send, recv_sem=recv, device_id=device, device_id_type=MESH
        )

    loads[0].wait()
    row = lax.broadcasted_iota(jnp.int32, (16, 128), 0)
    wanted = jnp.full((16, 128), -1, jnp.int32)
    for leaf in range(2):
        for n in range(NEAR):
            wanted = jnp.where(row == leaf * NEAR + n, near[leaf, n], wanted)
    asked[gy] = wanted.astype(F32).astype(BF16)
    for load in loads[1:]:
        load.wait()

    @pl.loop(0, 2)
    def _(leaf):
        at = pl.ds(pl.multiple_of(leaf * LEAF, LEAF), LEAF)
        wide = points[:, at].astype(F32)
        rows = square_rows(wide)
        own_right[leaf, 0:D] = points[:, at]
        own_right[leaf, D:AUG] = rows.astype(BF16)
        both = jnp.concatenate([wide, turned(rows), jnp.zeros((48, LEAF), F32)], axis=0)
        own_left[leaf] = both.T.astype(BF16)
        own[leaf, 0:D] = points[:, at]
        own[leaf, D:LEAF_ROWS] = residual[:, at].astype(BF16)

    place = lax.broadcasted_iota(jnp.int32, (CPD, RANK), 0)
    skel = dot(points[...], jnp.where(place == skeleton[...], 1.0, 0.0).astype(BF16))
    rows = square_rows(skel)
    left = jnp.concatenate([skel, turned(rows), jnp.zeros((48, RANK), F32)], axis=0).T.astype(BF16)
    weights = jnp.zeros((NRHS, RANK), F32)
    for leaf in range(2):
        tile = jnp.exp2(SCALE * dot(left[:, :AUG], own_right[leaf]))
        weights += dot(residual[:, pl.ds(leaf * LEAF, LEAF)], tile, ((1,), (1,)), FULL)
    mine = FIRST + me
    nodes[mine, 0:D] = skel.astype(BF16)
    nodes[mine, D:AUG] = rows.astype(BF16)
    nodes[mine, AUG:PAY] = (weights * (1.0 / math.sqrt(CPD))).astype(BF16)

    pl.semaphore_wait(barrier, N_GY - 1 + N_GX - 1)

    def req_copy(peer, slot):
        return copy(asked.at[gy], asked.at[slot], req_s.at[peer], req_r.at[slot], (gx, peer))

    def pay_copy(peer, slot):
        at = FIRST + gx * N_GY + slot
        return copy(nodes.at[mine], nodes.at[at], pay_s.at[peer], pay_r.at[slot], (gx, peer))

    def near_copy(peer, slot):
        return copy(stage.at[peer], leaves.at[slot], near_s.at[peer], near_r.at[slot], (gx, peer))

    @pl.loop(1, N_GY)
    def _(k):
        req_copy((gy + k) % N_GY, gy).start()

    @pl.loop(1, N_GY)
    def _(k):
        pay_copy((gy + k) % N_GY, gy).start()

    this = (2 * me + 1).astype(F32)
    leaves[gy] = own[0]

    @pl.loop(1, N_GY)
    def _(k):
        peer = (gy + k) % N_GY
        req_copy(peer, peer).wait_recv()
        second = jnp.where(asked[peer].astype(F32) == this, 1.0, 0.0)
        second = jnp.max(second, axis=0, keepdims=True)
        second = jnp.concatenate([second] * 4, axis=1)
        for r in range(0, LEAF_ROWS, 32):
            at = pl.ds(r, 32)
            stage[peer, at] = jnp.where(
                jnp.broadcast_to(second, (32, LEAF)) > 0.5, own[1, at].astype(F32), own[0, at].astype(F32)
            ).astype(BF16)
        near_copy(peer, gy).start()

    def tile_term(leaf, right, values):
        tile = jnp.exp2(SCALE * dot(own_left[leaf, :, :AUG], right)).astype(BF16)
        return dot(tile, values, ((1,), (1,)))

    @pl.loop(0, 2)
    def _(leaf):
        near_acc[leaf] = tile_term(leaf, own_right[leaf], own[leaf, D:LEAF_ROWS])

    @pl.loop(1, N_GY)
    def _(k):
        peer = (gy + k) % N_GY
        pay_copy(peer, peer).wait_recv()

    def half(row, h):
        return nodes.at[pl.ds(FIRST + row * N_GY + h * 8, 8)]

    def row_of(step, other=False):
        return 2 * ((y + step) % N_Y) + (1 - core if other else core)

    def y_copy(step, h, source):
        to = (row_of(step), gy)
        k = 0 if step == 1 else 1
        return copy(half(gx, h), half(row_of(source), h), y_s.at[k, h], y_r.at[k, h], to)

    def on_copy(step, source):
        h = k = 0 if step == 1 else 1
        return copy(half(row_of(-step), h), half(row_of(source), h), on_s.at[k], on_r.at[k], (row_of(step), gy))

    def sib_copy(step, h, other):
        at = (y + step) % N_Y
        return copy(half(row_of(step), h), half(row_of(step, other), h), sib_s.at[at, h], sib_r.at[at, h], (sibling, gy))

    for h in range(2):
        y_copy(1, h, 0).start()
        y_copy(-1, 1 - h, 0).start()
    for h in range(2):
        sib_copy(0, h, False).start()

    def build(first, count):
        done = []
        for i in range(count):
            u = first + i
            a, b = nodes[2 * u + 1], nodes[2 * u + 2]
            choice = jnp.broadcast_to(upper[pl.ds(u, 1), :], (AUG, RANK))
            lane = jnp.bitwise_and(choice, RANK - 1)
            from_a, from_b = (
                jnp.take_along_axis(x[:AUG].astype(F32), lane, axis=1, mode="promise_in_bounds") for x in (a, b)
            )
            right = jnp.where(choice < RANK, from_a, from_b)
            left = jnp.concatenate([right[:D], turned(right[D:])], axis=0).astype(BF16)
            both = jnp.concatenate([a, b], axis=1)
            tile = jnp.exp2(SCALE * dot(left, both[:AUG], ((0,), (0,)))).astype(BF16)
            sums = dot(both[D:], tile, ((1,), (1,)))
            done.append((right.astype(BF16), (sums[16:] / sums[4:5]).astype(BF16)))
        for i, (right, weights) in enumerate(done):
            nodes[first + i, 0:AUG] = right
            nodes[first + i, AUG:PAY] = weights

    def build_row(row):
        build(63 + row * 8, 8)
        build(31 + row * 4, 4)
        build(15 + row * 2, 2)
        build(7 + row, 1)

    def near_tile(n):
        leaf, pair = n // (NEAR // 2), n % (NEAR // 2)
        got = [leaves[(near[leaf, 2 * pair + i] // 2) % N_GY] for i in range(2)]
        got = jnp.concatenate(got, axis=1)
        right = jnp.concatenate([got[:D], square_rows(got[:D].astype(F32)).astype(BF16)], axis=0)
        near_acc[leaf] = near_acc[leaf] + tile_term(leaf, right, got[D:])

    @pl.loop(0, N_GX)
    def _(i):
        @pl.when(i == 1)
        def _():
            for step in (1, -1):
                h = 0 if step == 1 else 1
                y_copy(step, h, -step).wait_recv()
                on_copy(step, -step).start()
                sib_copy(-step, h, False).start()
            for h in range(2):
                sib_copy(0, h, True).wait_recv()

        @pl.when(i == 2)
        def _():
            for step in (-1, 1):
                h = 1 if step == 1 else 0
                y_copy(step, h, -step).wait_recv()
                sib_copy(-step, h, False).start()

        @pl.when(i == 3)
        def _():
            for h in range(2):
                sib_copy(1, h, True).wait_recv()

        @pl.when(i == 5)
        def _():
            for h in range(2):
                sib_copy(-1, h, True).wait_recv()

        @pl.when(i == 6)
        def _():
            for step in (1, -1):
                on_copy(step, 2).wait_recv()
                sib_copy(2, 0 if step == 1 else 1, False).start()

        @pl.when(i == 7)
        def _():
            for h in range(2):
                sib_copy(2, h, True).wait_recv()

        turn = i // 2
        away = turn + turn // 2 - 2 * (turn // 3)
        build_row(2 * ((y + away) % N_Y) + (core + i % 2) % 2)

    build(3, 4)
    build(1, 2)
    build(0, 1)

    far_acc[...] = jnp.zeros_like(far_acc)

    @pl.loop(0, FAR // 4)
    def _(n):
        leaf, group = n // (FAR // 8), n % (FAR // 8)
        got = jnp.concatenate([nodes[far[leaf, 8 * group + i]] for i in range(8)], axis=1)
        far_acc[leaf] = far_acc[leaf] + tile_term(leaf, got[:AUG], got[AUG:])

    @pl.loop(1, N_GY)
    def _(k):
        peer = (gy + k) % N_GY
        near_copy(peer, peer).wait_recv()

    pl.loop(0, NEAR)(near_tile)

    for leaf in range(2):
        at = pl.ds(leaf * LEAF, LEAF)
        terms = near_acc[leaf] * (1.0 / math.sqrt(LEAF)) + far_acc[leaf] * (1.0 / RANK)
        image[:, at] = residual[:, at] + terms.T

    both = jnp.concatenate([image[...], residual[...]], axis=0)
    gram = dot(image[...], both, ((1,), (1,)), FULL)
    part1[gy] = jnp.concatenate([gram[:16], gram[16:]], axis=1)

    def one_copy(peer, slot):
        return copy(part1.at[gy], part1.at[slot], one_s.at[peer], one_r.at[slot], (gx, peer))

    def two_copy(peer, slot):
        return copy(part2.at[gx], part2.at[slot], two_s.at[peer], two_r.at[slot], (peer, gy))

    @pl.loop(1, N_GY)
    def _(k):
        one_copy((gy + k) % N_GY, gy).start()

    @pl.loop(1, N_GY)
    def _(k):
        peer = (gy + k) % N_GY
        one_copy(peer, peer).wait_recv()

    total = part1[0]
    for k in range(1, N_GY):
        total += part1[k]
    part2[gx] = total

    @pl.loop(1, N_GX)
    def _(k):
        two_copy((gx + k) % N_GX, gx).start()

    @pl.loop(1, N_GX)
    def _(k):
        peer = (gx + k) % N_GX
        two_copy(peer, peer).wait_recv()

    total = part2[0]
    for k in range(1, N_GX):
        total += part2[k]

    work = jnp.concatenate([total, pltpu.roll(total, 64, 1)], axis=0)
    row = lax.broadcasted_iota(jnp.int32, (NRHS, 128), 0)

    def eight(_, work):
        for k in range(0, 8, 2):
            first, second = (jnp.broadcast_to(work[:, k + i : k + i + 1], (NRHS, 128)) for i in range(2))
            inverse = 1.0 / first[k : k + 1]
            factor = first[k + 1 : k + 2] * inverse
            below = 1.0 / (second[k + 1 : k + 2] - factor * second[k : k + 1])
            lower = (work[k + 1 : k + 2] - factor * work[k : k + 1]) * below
            upper_row = (work[k : k + 1] - second[k : k + 1] * lower) * inverse
            rest = work - first * upper_row - second * lower
            work = jnp.where(row == k, upper_row, jnp.where(row == k + 1, lower, rest))
        return pltpu.roll(jnp.concatenate([work[8:], work[:8]], axis=0), 120, 1)

    work = lax.fori_loop(0, NRHS // 8, eight, work)
    coeffs[...] = work

    @pl.loop(1, N_GY)
    def _(k):
        peer = (gy + k) % N_GY
        req_copy(peer, gy).wait_send()
        pay_copy(peer, gy).wait_send()
        near_copy(peer, gy).wait_send()
        one_copy(peer, gy).wait_send()

    @pl.loop(1, N_GX)
    def _(k):
        two_copy((gx + k) % N_GX, gx).wait_send()

    for step in (1, -1):
        for h in range(2):
            y_copy(step, h, 0).wait_send()
        on_copy(step, -step).wait_send()
    for step in range(N_Y):
        for h in range(2):
            sib_copy(step, h, False).wait_send()


def update_body(work, solution, residual, image, solution_next, residual_next, image_out):
    step = work[:, :NRHS].T
    solution_next[...] = solution[...] + dot(step, residual[...], precision=FULL)
    residual_next[...] = residual[...] - dot(step, image[...], precision=FULL)
    image_out[...] = image[...]


def shards(points, solution, residual, near_leaves, node_skeleton, upper_skeleton, far_nodes):
    vmem, hbm = (pl.BlockSpec(memory_space=m) for m in (pltpu.VMEM, pltpu.HBM))
    dma = pltpu.SemaphoreType.DMA
    residual_t = residual.T
    image_t, work = pl.pallas_call(
        kernel_body,
        out_shape=(
            jax.ShapeDtypeStruct((NRHS, CPD), F32),
            jax.ShapeDtypeStruct((NRHS, 128), F32),
        ),
        in_specs=[hbm] * 6,
        out_specs=(vmem, vmem),
        scratch_shapes=[
            pltpu.VMEM((D, CPD), BF16),
            pltpu.VMEM((NRHS, CPD), F32),
            pltpu.SMEM((2, NEAR), jnp.int32),
            pltpu.VMEM((1, RANK), jnp.int32),
            pltpu.VMEM((FIRST, RANK), jnp.int32),
            pltpu.SMEM((2, FAR), jnp.int32),
            pltpu.VMEM((NODES, PAY, RANK), BF16),
            pltpu.VMEM((2, LEAF_ROWS, LEAF), BF16),
            pltpu.VMEM((2, AUG, LEAF), BF16),
            pltpu.VMEM((2, LEAF, 128), BF16),
            pltpu.VMEM((N_GY, 16, 128), BF16),
            pltpu.VMEM((N_GY, LEAF_ROWS, LEAF), BF16),
            pltpu.VMEM((N_GY, LEAF_ROWS, LEAF), BF16),
            pltpu.VMEM((2, LEAF, NRHS), F32),
            pltpu.VMEM((2, LEAF, NRHS), F32),
            pltpu.VMEM((N_GY, 16, 128), F32),
            pltpu.VMEM((N_GX, 16, 128), F32),
            dma((6,)),
            dma((N_GY,)), dma((N_GY,)), dma((N_GY,)), dma((N_GY,)), dma((N_GY,)), dma((N_GY,)),
            dma((2, 2)), dma((2, 2)), dma((2,)), dma((2,)), dma((N_Y, 2)), dma((N_Y, 2)),
            dma((N_GY,)), dma((N_GY,)), dma((N_GX,)), dma((N_GX,)),
        ],
        compiler_params=pltpu.CompilerParams(
            collective_id=0, has_side_effects=True, vmem_limit_bytes=60 * 2**20
        ),
    )(points.T, residual_t, near_leaves, node_skeleton, upper_skeleton, far_nodes)
    outs = pl.pallas_call(
        update_body,
        out_shape=(jax.ShapeDtypeStruct((NRHS, CPD), F32),) * 3,
        in_specs=[vmem] * 4,
        out_specs=(vmem,) * 3,
    )(work, solution.T, residual_t, image_t)
    return tuple(o.T for o in outs)


def solution(mesh):
    split = P(("gx", "gy"), None)
    return jax.shard_map(
        shards,
        mesh=mesh,
        in_specs=(split, split, split, split, split, P(), split),
        out_specs=(split, split, split),
        check_vma=False,
    )
```

```python
import math

import jax
import jax.numpy as jnp
from jax import lax
from jax.experimental import pallas as pl
from jax.experimental.pallas import tpu as pltpu
from jax.sharding import PartitionSpec as P

D = 64
NRHS = 32
LEAF = 512
RANK = 128
NEAR = 4
FAR = 16
CPD = 1024
N_GX = 8
N_GY = 16
N_Y = 4
NODES = 255
FIRST = 127
AUG = D + 16
SENT = D + NRHS
PAY = SENT + 16
LEAF_ROWS = D + NRHS
SCALE = math.log2(math.e) / D
FULL = lax.Precision.HIGHEST
F32, BF16 = jnp.float32, jnp.bfloat16
MESH = pl.DeviceIdType.MESH


def dot(a, b, contract=((1,), (0,)), precision=None):
    return lax.dot_general(a, b, (contract, ((), ())), precision=precision, preferred_element_type=F32)


def square_rows(wide):
    half = -0.5 * jnp.sum(wide * wide, axis=0, keepdims=True)
    high = half.astype(BF16).astype(F32)
    rest = half - high
    middle = rest.astype(BF16).astype(F32)
    low = rest - middle
    row = lax.broadcasted_iota(jnp.int32, (16, wide.shape[1]), 0)
    ones = jnp.where((row >= 4) & (row < 7), 1.0, 0.0)
    return jnp.where(row == 0, high, jnp.where(row == 1, middle, jnp.where(row == 2, low, ones)))


def turned(rows):
    return jnp.concatenate([pltpu.roll(rows[:8], 4, 0), rows[8:]], axis=0)


def kernel_body(
    points_in, residual_in, near_in, skeleton_in, upper_in, far_in,
    image, coeffs,
    points, residual, near, skeleton, upper, far,
    nodes, own, own_right, own_left, asked, stage, leaves, near_acc, far_acc, part1, part2,
    in_s, req_s, req_r, pay_s, pay_r, near_s, near_r, y_s, y_r, on_s, on_r, sib_s, sib_r,
    one_s, one_r, two_s, two_r,
):
    gx, gy = lax.axis_index("gx"), lax.axis_index("gy")
    y, core = gx // 2, gx % 2
    me = gx * N_GY + gy
    sibling = 2 * y + (1 - core)

    pairs = ((near_in, near), (skeleton_in, skeleton), (points_in, points), (residual_in, residual), (upper_in, upper), (far_in, far))
    loads = [pltpu.make_async_copy(a, b, in_s.at[i]) for i, (a, b) in enumerate(pairs)]
    for load in loads:
        load.start()

    barrier = pltpu.get_barrier_semaphore()

    @pl.loop(1, N_GY)
    def _(k):
        pl.semaphore_signal(barrier, inc=1, device_id=(gx, (gy + k) % N_GY), device_id_type=MESH)

    @pl.loop(1, N_GX)
    def _(k):
        pl.semaphore_signal(barrier, inc=1, device_id=((gx + k) % N_GX, gy), device_id_type=MESH)

    def copy(src, dst, send, recv, device):
        return pltpu.make_async_remote_copy(
            src_ref=src, dst_ref=dst, send_sem=send, recv_sem=recv, device_id=device, device_id_type=MESH
        )

    loads[0].wait()
    row = lax.broadcasted_iota(jnp.int32, (16, 128), 0)
    wanted = jnp.full((16, 128), -1, jnp.int32)
    for leaf in range(2):
        for n in range(NEAR):
            wanted = jnp.where(row == leaf * NEAR + n, near[leaf, n], wanted)
    asked[gy] = wanted.astype(F32).astype(BF16)
    for load in loads[1:]:
        load.wait()

    @pl.loop(0, 2)
    def _(leaf):
        at = pl.ds(pl.multiple_of(leaf * LEAF, LEAF), LEAF)
        wide = points[:, at].astype(F32)
        rows = square_rows(wide)
        own_right[leaf, 0:D] = points[:, at]
        own_right[leaf, D:AUG] = rows.astype(BF16)
        both = jnp.concatenate([wide, turned(rows), jnp.zeros((48, LEAF), F32)], axis=0)
        own_left[leaf] = both.T.astype(BF16)
        own[leaf, 0:D] = points[:, at]
        own[leaf, D:LEAF_ROWS] = residual[:, at].astype(BF16)

    place = lax.broadcasted_iota(jnp.int32, (CPD, RANK), 0)
    skel = dot(points[...], jnp.where(place == skeleton[...], 1.0, 0.0).astype(BF16))
    rows = square_rows(skel)
    left = jnp.concatenate([skel, turned(rows), jnp.zeros((48, RANK), F32)], axis=0).T.astype(BF16)
    weights = jnp.zeros((NRHS, RANK), F32)
    for leaf in range(2):
        tile = jnp.exp2(SCALE * dot(left[:, :AUG], own_right[leaf]))
        weights += dot(residual[:, pl.ds(leaf * LEAF, LEAF)], tile, ((1,), (1,)), FULL)
    mine = FIRST + me
    nodes[mine, 0:D] = skel.astype(BF16)
    nodes[mine, D:SENT] = (weights * (1.0 / math.sqrt(CPD))).astype(BF16)

    pl.semaphore_wait(barrier, N_GY - 1 + N_GX - 1)

    def req_copy(peer, slot):
        return copy(asked.at[gy], asked.at[slot], req_s.at[peer], req_r.at[slot], (gx, peer))

    def pay_copy(peer, slot):
        at = FIRST + gx * N_GY + slot
        return copy(nodes.at[mine, pl.ds(0, SENT)], nodes.at[at, pl.ds(0, SENT)], pay_s.at[peer], pay_r.at[slot], (gx, peer))

    def near_copy(peer, slot):
        return copy(stage.at[peer], leaves.at[slot], near_s.at[peer], near_r.at[slot], (gx, peer))

    @pl.loop(1, N_GY)
    def _(k):
        req_copy((gy + k) % N_GY, gy).start()

    @pl.loop(1, N_GY)
    def _(k):
        pay_copy((gy + k) % N_GY, gy).start()

    def tile_term(leaf, right, values):
        tile = jnp.exp2(SCALE * dot(own_left[leaf, :, :AUG], right)).astype(BF16)
        return dot(tile, values, ((1,), (1,)))

    @pl.loop(0, 2)
    def _(leaf):
        near_acc[leaf] = tile_term(leaf, own_right[leaf], own[leaf, D:LEAF_ROWS])

    @pl.loop(1, N_GY)
    def _(k):
        peer = (gy + k) % N_GY
        pay_copy(peer, peer).wait_recv()

    def half(row, h):
        return nodes.at[pl.ds(FIRST + row * N_GY + h * 8, 8), pl.ds(0, SENT)]

    def row_of(step, other=False):
        return 2 * ((y + step) % N_Y) + (1 - core if other else core)

    def y_copy(step, h, source):
        to = (row_of(step), gy)
        k = 0 if step == 1 else 1
        return copy(half(gx, h), half(row_of(source), h), y_s.at[k, h], y_r.at[k, h], to)

    def on_copy(step, source):
        h = k = 0 if step == 1 else 1
        return copy(half(row_of(-step), h), half(row_of(source), h), on_s.at[k], on_r.at[k], (row_of(step), gy))

    def sib_copy(step, h, other):
        at = (y + step) % N_Y
        return copy(half(row_of(step), h), half(row_of(step, other), h), sib_s.at[at, h], sib_r.at[at, h], (sibling, gy))

    for h in range(2):
        y_copy(1, h, 0).start()
        y_copy(-1, 1 - h, 0).start()
    for h in range(2):
        sib_copy(0, h, False).start()

    this = (2 * me + 1).astype(F32)
    leaves[gy] = own[0]

    @pl.loop(1, N_GY)
    def _(k):
        peer = (gy + k) % N_GY
        req_copy(peer, peer).wait_recv()
        second = jnp.where(asked[peer].astype(F32) == this, 1.0, 0.0)
        second = jnp.max(second, axis=0, keepdims=True)
        second = jnp.concatenate([second] * 4, axis=1)
        for r in range(0, LEAF_ROWS, 32):
            at = pl.ds(r, 32)
            stage[peer, at] = jnp.where(
                jnp.broadcast_to(second, (32, LEAF)) > 0.5, own[1, at].astype(F32), own[0, at].astype(F32)
            ).astype(BF16)
        near_copy(peer, gy).start()

    def right_of(node):
        return jnp.concatenate([node[:D], node[SENT:]], axis=0)

    def build(first, count):
        done = []
        for i in range(count):
            u = first + i
            a, b = nodes[2 * u + 1], nodes[2 * u + 2]
            choice = jnp.broadcast_to(upper[pl.ds(u, 1), :], (AUG, RANK))
            lane = jnp.bitwise_and(choice, RANK - 1)
            from_a, from_b = (
                jnp.take_along_axis(right_of(x).astype(F32), lane, axis=1, mode="promise_in_bounds") for x in (a, b)
            )
            right = jnp.where(choice < RANK, from_a, from_b)
            left = jnp.concatenate([right[:D], turned(right[D:])], axis=0).astype(BF16)
            both = jnp.concatenate([a, b], axis=1)
            tile = jnp.exp2(SCALE * dot(left, right_of(both), ((0,), (0,)))).astype(BF16)
            sums = dot(both[D:], tile, ((1,), (1,)))
            weights = sums[:NRHS] / sums[NRHS + 4 : NRHS + 5]
            done.append(jnp.concatenate([right[:D], weights, right[D:]], axis=0).astype(BF16))
        for i, node in enumerate(done):
            nodes[first + i] = node

    def build_row(row):
        for h in range(2):
            first = FIRST + row * N_GY + h * 8
            wide = jnp.concatenate([nodes[first + i, 0:D].astype(F32) for i in range(8)], axis=1)
            rows = square_rows(wide).astype(BF16)
            for i in range(8):
                nodes[first + i, SENT:PAY] = rows[:, i * RANK : (i + 1) * RANK]
        build(63 + row * 8, 8)
        build(31 + row * 4, 4)
        build(15 + row * 2, 2)
        build(7 + row, 1)

    def near_tile(n):
        leaf, pair = n // (NEAR // 2), n % (NEAR // 2)
        got = [leaves[(near[leaf, 2 * pair + i] // 2) % N_GY] for i in range(2)]
        got = jnp.concatenate(got, axis=1)
        right = jnp.concatenate([got[:D], square_rows(got[:D].astype(F32)).astype(BF16)], axis=0)
        near_acc[leaf] = near_acc[leaf] + tile_term(leaf, right, got[D:])

    @pl.loop(0, N_GX)
    def _(i):
        @pl.when(i == 1)
        def _():
            for step in (1, -1):
                h = 0 if step == 1 else 1
                y_copy(step, h, -step).wait_recv()
                on_copy(step, -step).start()
                sib_copy(-step, h, False).start()
            for h in range(2):
                sib_copy(0, h, True).wait_recv()

        @pl.when(i == 2)
        def _():
            for step in (-1, 1):
                h = 1 if step == 1 else 0
                y_copy(step, h, -step).wait_recv()
                sib_copy(-step, h, False).start()

        @pl.when(i == 3)
        def _():
            for h in range(2):
                sib_copy(1, h, True).wait_recv()

        @pl.when(i == 5)
        def _():
            for h in range(2):
                sib_copy(-1, h, True).wait_recv()

        @pl.when(i == 6)
        def _():
            for step in (1, -1):
                on_copy(step, 2).wait_recv()
                sib_copy(2, 0 if step == 1 else 1, False).start()

        @pl.when(i == 7)
        def _():
            for h in range(2):
                sib_copy(2, h, True).wait_recv()

        turn = i // 2
        away = turn + turn // 2 - 2 * (turn // 3)
        build_row(2 * ((y + away) % N_Y) + (core + i % 2) % 2)

    build(3, 4)
    build(1, 2)
    build(0, 1)

    far_acc[...] = jnp.zeros_like(far_acc)

    @pl.loop(0, FAR // 4)
    def _(n):
        leaf, group = n // (FAR // 8), n % (FAR // 8)
        got = jnp.concatenate([nodes[far[leaf, 8 * group + i]] for i in range(8)], axis=1)
        far_acc[leaf] = far_acc[leaf] + tile_term(leaf, right_of(got), got[D:SENT])

    @pl.loop(1, N_GY)
    def _(k):
        peer = (gy + k) % N_GY
        near_copy(peer, peer).wait_recv()

    pl.loop(0, NEAR)(near_tile)

    for leaf in range(2):
        at = pl.ds(leaf * LEAF, LEAF)
        terms = near_acc[leaf] * (1.0 / math.sqrt(LEAF)) + far_acc[leaf] * (1.0 / RANK)
        image[:, at] = residual[:, at] + terms.T

    both = jnp.concatenate([image[...], residual[...]], axis=0)
    gram = dot(image[...], both, ((1,), (1,)), FULL)
    part1[gy] = jnp.concatenate([gram[:16], gram[16:]], axis=1)

    def one_copy(peer, slot):
        return copy(part1.at[gy], part1.at[slot], one_s.at[peer], one_r.at[slot], (gx, peer))

    def two_copy(peer, slot):
        return copy(part2.at[gx], part2.at[slot], two_s.at[peer], two_r.at[slot], (peer, gy))

    @pl.loop(1, N_GY)
    def _(k):
        one_copy((gy + k) % N_GY, gy).start()

    @pl.loop(1, N_GY)
    def _(k):
        peer = (gy + k) % N_GY
        one_copy(peer, peer).wait_recv()

    total = part1[0]
    for k in range(1, N_GY):
        total += part1[k]
    part2[gx] = total

    @pl.loop(1, N_GX)
    def _(k):
        two_copy((gx + k) % N_GX, gx).start()

    @pl.loop(1, N_GX)
    def _(k):
        peer = (gx + k) % N_GX
        two_copy(peer, peer).wait_recv()

    total = part2[0]
    for k in range(1, N_GX):
        total += part2[k]

    work = jnp.concatenate([total, pltpu.roll(total, 64, 1)], axis=0)
    row = lax.broadcasted_iota(jnp.int32, (NRHS, 128), 0)

    def eight(_, work):
        for k in range(0, 8, 2):
            first, second = (jnp.broadcast_to(work[:, k + i : k + i + 1], (NRHS, 128)) for i in range(2))
            inverse = 1.0 / first[k : k + 1]
            factor = first[k + 1 : k + 2] * inverse
            below = 1.0 / (second[k + 1 : k + 2] - factor * second[k : k + 1])
            lower = (work[k + 1 : k + 2] - factor * work[k : k + 1]) * below
            upper_row = (work[k : k + 1] - second[k : k + 1] * lower) * inverse
            rest = work - first * upper_row - second * lower
            work = jnp.where(row == k, upper_row, jnp.where(row == k + 1, lower, rest))
        return pltpu.roll(jnp.concatenate([work[8:], work[:8]], axis=0), 120, 1)

    work = lax.fori_loop(0, NRHS // 8, eight, work)
    coeffs[...] = work

    @pl.loop(1, N_GY)
    def _(k):
        peer = (gy + k) % N_GY
        req_copy(peer, gy).wait_send()
        pay_copy(peer, gy).wait_send()
        near_copy(peer, gy).wait_send()
        one_copy(peer, gy).wait_send()

    @pl.loop(1, N_GX)
    def _(k):
        two_copy((gx + k) % N_GX, gx).wait_send()

    for step in (1, -1):
        for h in range(2):
            y_copy(step, h, 0).wait_send()
        on_copy(step, -step).wait_send()
    for step in range(N_Y):
        for h in range(2):
            sib_copy(step, h, False).wait_send()


def update_body(work, solution, residual, image, solution_next, residual_next, image_out):
    step = work[:, :NRHS].T
    solution_next[...] = solution[...] + dot(step, residual[...], precision=FULL)
    residual_next[...] = residual[...] - dot(step, image[...], precision=FULL)
    image_out[...] = image[...]


def shards(points, solution, residual, near_leaves, node_skeleton, upper_skeleton, far_nodes):
    vmem, hbm = (pl.BlockSpec(memory_space=m) for m in (pltpu.VMEM, pltpu.HBM))
    dma = pltpu.SemaphoreType.DMA
    residual_t = residual.T
    image_t, work = pl.pallas_call(
        kernel_body,
        out_shape=(
            jax.ShapeDtypeStruct((NRHS, CPD), F32),
            jax.ShapeDtypeStruct((NRHS, 128), F32),
        ),
        in_specs=[hbm] * 6,
        out_specs=(vmem, vmem),
        scratch_shapes=[
            pltpu.VMEM((D, CPD), BF16),
            pltpu.VMEM((NRHS, CPD), F32),
            pltpu.SMEM((2, NEAR), jnp.int32),
            pltpu.VMEM((1, RANK), jnp.int32),
            pltpu.VMEM((FIRST, RANK), jnp.int32),
            pltpu.SMEM((2, FAR), jnp.int32),
            pltpu.VMEM((NODES, PAY, RANK), BF16),
            pltpu.VMEM((2, LEAF_ROWS, LEAF), BF16),
            pltpu.VMEM((2, AUG, LEAF), BF16),
            pltpu.VMEM((2, LEAF, 128), BF16),
            pltpu.VMEM((N_GY, 16, 128), BF16),
            pltpu.VMEM((N_GY, LEAF_ROWS, LEAF), BF16),
            pltpu.VMEM((N_GY, LEAF_ROWS, LEAF), BF16),
            pltpu.VMEM((2, LEAF, NRHS), F32),
            pltpu.VMEM((2, LEAF, NRHS), F32),
            pltpu.VMEM((N_GY, 16, 128), F32),
            pltpu.VMEM((N_GX, 16, 128), F32),
            dma((6,)),
            dma((N_GY,)), dma((N_GY,)), dma((N_GY,)), dma((N_GY,)), dma((N_GY,)), dma((N_GY,)),
            dma((2, 2)), dma((2, 2)), dma((2,)), dma((2,)), dma((N_Y, 2)), dma((N_Y, 2)),
            dma((N_GY,)), dma((N_GY,)), dma((N_GX,)), dma((N_GX,)),
        ],
        compiler_params=pltpu.CompilerParams(
            collective_id=0, has_side_effects=True, vmem_limit_bytes=60 * 2**20
        ),
    )(points.T, residual_t, near_leaves, node_skeleton, upper_skeleton, far_nodes)
    outs = pl.pallas_call(
        update_body,
        out_shape=(jax.ShapeDtypeStruct((NRHS, CPD), F32),) * 3,
        in_specs=[vmem] * 4,
        out_specs=(vmem,) * 3,
    )(work, solution.T, residual_t, image_t)
    return tuple(o.T for o in outs)


def solution(mesh):
    split = P(("gx", "gy"), None)
    return jax.shard_map(
        shards,
        mesh=mesh,
        in_specs=(split, split, split, split, split, P(), split),
        out_specs=(split, split, split),
        check_vma=False,
    )
```

```python
import math

import jax
import jax.numpy as jnp
from jax import lax
from jax.experimental import pallas as pl
from jax.experimental.pallas import tpu as pltpu
from jax.sharding import PartitionSpec as P

D = 64
NRHS = 32
LEAF = 512
RANK = 128
NEAR = 4
FAR = 16
CPD = 1024
N_GX = 8
N_GY = 16
N_Y = 4
NODES = 255
FIRST = 127
AUG = D + 16
SENT = D + NRHS
PAY = SENT + 16
LEAF_ROWS = D + NRHS
SCALE = math.log2(math.e) / D
FULL = lax.Precision.HIGHEST
F32, BF16 = jnp.float32, jnp.bfloat16
MESH = pl.DeviceIdType.MESH


def dot(a, b, contract=((1,), (0,)), precision=None):
    return lax.dot_general(a, b, (contract, ((), ())), precision=precision, preferred_element_type=F32)


def square_rows(wide):
    half = -0.5 * jnp.sum(wide * wide, axis=0, keepdims=True)
    high = half.astype(BF16).astype(F32)
    rest = half - high
    middle = rest.astype(BF16).astype(F32)
    low = rest - middle
    row = lax.broadcasted_iota(jnp.int32, (16, wide.shape[1]), 0)
    ones = jnp.where((row >= 4) & (row < 7), 1.0, 0.0)
    return jnp.where(row == 0, high, jnp.where(row == 1, middle, jnp.where(row == 2, low, ones)))


def turned(rows):
    return jnp.concatenate([pltpu.roll(rows[:8], 4, 0), rows[8:]], axis=0)


def kernel_body(
    points_in, residual_in, near_in, skeleton_in, upper_in, far_in,
    image, coeffs,
    points, residual, near, skeleton, upper, far,
    nodes, own, own_right, own_left, asked, stage, leaves, near_acc, far_acc, part1, part2,
    in_s, req_s, req_r, pay_s, pay_r, near_s, near_r, y_s, y_r, on_s, on_r, sib_s, sib_r, full_s, full_r,
    one_s, one_r, two_s, two_r,
):
    gx, gy = lax.axis_index("gx"), lax.axis_index("gy")
    y, core = gx // 2, gx % 2
    me = gx * N_GY + gy
    sibling = 2 * y + (1 - core)

    pairs = ((near_in, near), (skeleton_in, skeleton), (points_in, points), (residual_in, residual), (upper_in, upper), (far_in, far))
    loads = [pltpu.make_async_copy(a, b, in_s.at[i]) for i, (a, b) in enumerate(pairs)]
    for load in loads:
        load.start()

    barrier = pltpu.get_barrier_semaphore()

    @pl.loop(1, N_GY)
    def _(k):
        pl.semaphore_signal(barrier, inc=1, device_id=(gx, (gy + k) % N_GY), device_id_type=MESH)

    @pl.loop(1, N_GX)
    def _(k):
        pl.semaphore_signal(barrier, inc=1, device_id=((gx + k) % N_GX, gy), device_id_type=MESH)

    def copy(src, dst, send, recv, device):
        return pltpu.make_async_remote_copy(
            src_ref=src, dst_ref=dst, send_sem=send, recv_sem=recv, device_id=device, device_id_type=MESH
        )

    loads[0].wait()
    row = lax.broadcasted_iota(jnp.int32, (16, 128), 0)
    wanted = jnp.full((16, 128), -1, jnp.int32)
    for leaf in range(2):
        for n in range(NEAR):
            wanted = jnp.where(row == leaf * NEAR + n, near[leaf, n], wanted)
    asked[gy] = wanted.astype(F32).astype(BF16)
    for load in loads[1:]:
        load.wait()

    @pl.loop(0, 2)
    def _(leaf):
        at = pl.ds(pl.multiple_of(leaf * LEAF, LEAF), LEAF)
        wide = points[:, at].astype(F32)
        rows = square_rows(wide)
        own_right[leaf, 0:D] = points[:, at]
        own_right[leaf, D:AUG] = rows.astype(BF16)
        both = jnp.concatenate([wide, turned(rows), jnp.zeros((48, LEAF), F32)], axis=0)
        own_left[leaf] = both.T.astype(BF16)
        own[leaf, 0:D] = points[:, at]
        own[leaf, D:LEAF_ROWS] = residual[:, at].astype(BF16)

    place = lax.broadcasted_iota(jnp.int32, (CPD, RANK), 0)
    skel = dot(points[...], jnp.where(place == skeleton[...], 1.0, 0.0).astype(BF16))
    rows = square_rows(skel)
    left = jnp.concatenate([skel, turned(rows), jnp.zeros((48, RANK), F32)], axis=0).T.astype(BF16)
    weights = jnp.zeros((NRHS, RANK), F32)
    for leaf in range(2):
        tile = jnp.exp2(SCALE * dot(left[:, :AUG], own_right[leaf]))
        weights += dot(residual[:, pl.ds(leaf * LEAF, LEAF)], tile, ((1,), (1,)), FULL)
    mine = FIRST + me
    nodes[mine, 0:D] = skel.astype(BF16)
    nodes[mine, D:SENT] = (weights * (1.0 / math.sqrt(CPD))).astype(BF16)

    pl.semaphore_wait(barrier, N_GY - 1 + N_GX - 1)

    def req_copy(peer, slot):
        return copy(asked.at[gy], asked.at[slot], req_s.at[peer], req_r.at[slot], (gx, peer))

    def pay_copy(peer, slot):
        at = FIRST + gx * N_GY + slot
        return copy(nodes.at[mine, pl.ds(0, SENT)], nodes.at[at, pl.ds(0, SENT)], pay_s.at[peer], pay_r.at[slot], (gx, peer))

    def near_copy(peer, slot):
        return copy(stage.at[peer], leaves.at[slot], near_s.at[peer], near_r.at[slot], (gx, peer))

    @pl.loop(1, N_GY)
    def _(k):
        req_copy((gy + k) % N_GY, gy).start()

    @pl.loop(1, N_GY)
    def _(k):
        pay_copy((gy + k) % N_GY, gy).start()

    def tile_term(leaf, right, values):
        tile = jnp.exp2(SCALE * dot(own_left[leaf, :, :AUG], right)).astype(BF16)
        return dot(tile, values, ((1,), (1,)))

    @pl.loop(0, 2)
    def _(leaf):
        near_acc[leaf] = tile_term(leaf, own_right[leaf], own[leaf, D:LEAF_ROWS])

    @pl.loop(1, N_GY)
    def _(k):
        peer = (gy + k) % N_GY
        pay_copy(peer, peer).wait_recv()

    def half(row, h):
        return nodes.at[pl.ds(FIRST + row * N_GY + h * 8, 8), pl.ds(0, SENT)]

    def row_of(step, other=False):
        return 2 * ((y + step) % N_Y) + (1 - core if other else core)

    def y_copy(step, h, source):
        to = (row_of(step), gy)
        k = 0 if step == 1 else 1
        return copy(half(gx, h), half(row_of(source), h), y_s.at[k, h], y_r.at[k, h], to)

    def on_copy(step, source):
        h = k = 0 if step == 1 else 1
        return copy(half(row_of(-step), h), half(row_of(source), h), on_s.at[k], on_r.at[k], (row_of(step), gy))

    def sib_copy(h, other):
        return copy(half(row_of(2), h), half(row_of(2, other), h), sib_s.at[h], sib_r.at[h], (sibling, gy))

    for h in range(2):
        y_copy(1, h, 0).start()
        y_copy(-1, 1 - h, 0).start()

    this = (2 * me + 1).astype(F32)
    leaves[gy] = own[0]

    @pl.loop(1, N_GY)
    def _(k):
        peer = (gy + k) % N_GY
        req_copy(peer, peer).wait_recv()
        second = jnp.where(asked[peer].astype(F32) == this, 1.0, 0.0)
        second = jnp.max(second, axis=0, keepdims=True)
        second = jnp.concatenate([second] * 4, axis=1)
        for r in range(0, LEAF_ROWS, 32):
            at = pl.ds(r, 32)
            stage[peer, at] = jnp.where(
                jnp.broadcast_to(second, (32, LEAF)) > 0.5, own[1, at].astype(F32), own[0, at].astype(F32)
            ).astype(BF16)
        near_copy(peer, gy).start()

    def right_of(node):
        return jnp.concatenate([node[:D], node[SENT:]], axis=0)

    def build(first, count):
        done = []
        for i in range(count):
            u = first + i
            a, b = nodes[2 * u + 1], nodes[2 * u + 2]
            choice = jnp.broadcast_to(upper[pl.ds(u, 1), :], (AUG, RANK))
            lane = jnp.bitwise_and(choice, RANK - 1)
            from_a, from_b = (
                jnp.take_along_axis(right_of(x).astype(F32), lane, axis=1, mode="promise_in_bounds") for x in (a, b)
            )
            right = jnp.where(choice < RANK, from_a, from_b)
            left = jnp.concatenate([right[:D], turned(right[D:])], axis=0).astype(BF16)
            both = jnp.concatenate([a, b], axis=1)
            tile = jnp.exp2(SCALE * dot(left, right_of(both), ((0,), (0,)))).astype(BF16)
            sums = dot(both[D:], tile, ((1,), (1,)))
            weights = sums[:NRHS] / sums[NRHS + 4 : NRHS + 5]
            done.append(jnp.concatenate([right[:D], weights, right[D:]], axis=0).astype(BF16))
        for i, node in enumerate(done):
            nodes[first + i] = node

    def build_row(row):
        for h in range(2):
            first = FIRST + row * N_GY + h * 8
            wide = jnp.concatenate([nodes[first + i, 0:D].astype(F32) for i in range(8)], axis=1)
            rows = square_rows(wide).astype(BF16)
            for i in range(8):
                nodes[first + i, SENT:PAY] = rows[:, i * RANK : (i + 1) * RANK]
        build(63 + row * 8, 8)
        build(31 + row * 4, 4)
        build(15 + row * 2, 2)
        build(7 + row, 1)

    def near_tile(n):
        leaf, pair = n // (NEAR // 2), n % (NEAR // 2)
        got = [leaves[(near[leaf, 2 * pair + i] // 2) % N_GY] for i in range(2)]
        got = jnp.concatenate(got, axis=1)
        right = jnp.concatenate([got[:D], square_rows(got[:D].astype(F32)).astype(BF16)], axis=0)
        near_acc[leaf] = near_acc[leaf] + tile_term(leaf, right, got[D:])

    def run(row, level):
        return nodes.at[pl.ds(2**level - 1 + row * (2**level // N_GX), 2**level // N_GX)]

    def full_copy(step, level, other):
        at = (y + step) % N_Y
        send, recv = full_s.at[at, level - 3], full_r.at[at, level - 3]
        return copy(run(row_of(step), level), run(row_of(step, other), level), send, recv, (sibling, gy))

    @pl.loop(0, N_Y + 1)
    def _(i):
        @pl.when(i == 1)
        def _():
            for step in (1, -1):
                h = 0 if step == 1 else 1
                y_copy(step, h, -step).wait_recv()
                on_copy(step, -step).start()
            y_copy(-1, 0, 1).wait_recv()

        @pl.when(i == 2)
        def _():
            y_copy(1, 1, -1).wait_recv()

        @pl.when(i == 3)
        def _():
            for step in (1, -1):
                on_copy(step, 2).wait_recv()
                sib_copy(0 if step == 1 else 1, False).start()

        @pl.when(i == 4)
        def _():
            for h in range(2):
                sib_copy(h, True).wait_recv()

        turn = i - i // N_Y
        away = turn + turn // 2 - 2 * (turn // 3)
        build_row(2 * ((y + away) % N_Y) + (core + i // N_Y) % 2)

        @pl.when(i < 3)
        def _():
            for level in range(7, 2, -1):
                full_copy(away, level, False).start()

    for step in (0, 1, -1):
        for level in range(7, 2, -1):
            full_copy(step, level, True).wait_recv()

    build(3, 4)
    build(1, 2)
    build(0, 1)

    far_acc[...] = jnp.zeros_like(far_acc)

    @pl.loop(0, FAR // 4)
    def _(n):
        leaf, group = n // (FAR // 8), n % (FAR // 8)
        got = jnp.concatenate([nodes[far[leaf, 8 * group + i]] for i in range(8)], axis=1)
        far_acc[leaf] = far_acc[leaf] + tile_term(leaf, right_of(got), got[D:SENT])

    @pl.loop(1, N_GY)
    def _(k):
        peer = (gy + k) % N_GY
        near_copy(peer, peer).wait_recv()

    pl.loop(0, NEAR)(near_tile)

    for leaf in range(2):
        at = pl.ds(leaf * LEAF, LEAF)
        terms = near_acc[leaf] * (1.0 / math.sqrt(LEAF)) + far_acc[leaf] * (1.0 / RANK)
        image[:, at] = residual[:, at] + terms.T

    both = jnp.concatenate([image[...], residual[...]], axis=0)
    gram = dot(image[...], both, ((1,), (1,)), FULL)
    part1[gy] = jnp.concatenate([gram[:16], gram[16:]], axis=1)

    def one_copy(peer, slot):
        return copy(part1.at[gy], part1.at[slot], one_s.at[peer], one_r.at[slot], (gx, peer))

    def two_copy(peer, slot):
        return copy(part2.at[gx], part2.at[slot], two_s.at[peer], two_r.at[slot], (peer, gy))

    @pl.loop(1, N_GY)
    def _(k):
        one_copy((gy + k) % N_GY, gy).start()

    @pl.loop(1, N_GY)
    def _(k):
        peer = (gy + k) % N_GY
        req_copy(peer, gy).wait_send()
        pay_copy(peer, gy).wait_send()
        near_copy(peer, gy).wait_send()

    for step in (1, -1):
        for h in range(2):
            y_copy(step, h, 0).wait_send()
        on_copy(step, -step).wait_send()
    for h in range(2):
        sib_copy(h, False).wait_send()

    @pl.loop(0, 3)
    def _(i):
        for level in range(7, 2, -1):
            full_copy(i - 1, level, False).wait_send()

    @pl.loop(1, N_GY)
    def _(k):
        peer = (gy + k) % N_GY
        one_copy(peer, peer).wait_recv()

    total = part1[0]
    for k in range(1, N_GY):
        total += part1[k]
    part2[gx] = total

    @pl.loop(1, N_GX)
    def _(k):
        two_copy((gx + k) % N_GX, gx).start()

    @pl.loop(1, N_GY)
    def _(k):
        one_copy((gy + k) % N_GY, gy).wait_send()

    @pl.loop(1, N_GX)
    def _(k):
        peer = (gx + k) % N_GX
        two_copy(peer, peer).wait_recv()

    total = part2[0]
    for k in range(1, N_GX):
        total += part2[k]

    work = jnp.concatenate([total, pltpu.roll(total, 64, 1)], axis=0)
    row = lax.broadcasted_iota(jnp.int32, (NRHS, 128), 0)

    def eight(_, work):
        for k in range(0, 8, 2):
            first, second = (jnp.broadcast_to(work[:, k + i : k + i + 1], (NRHS, 128)) for i in range(2))
            inverse = 1.0 / first[k : k + 1]
            factor = first[k + 1 : k + 2] * inverse
            below = 1.0 / (second[k + 1 : k + 2] - factor * second[k : k + 1])
            lower = (work[k + 1 : k + 2] - factor * work[k : k + 1]) * below
            upper_row = (work[k : k + 1] - second[k : k + 1] * lower) * inverse
            rest = work - first * upper_row - second * lower
            work = jnp.where(row == k, upper_row, jnp.where(row == k + 1, lower, rest))
        return pltpu.roll(jnp.concatenate([work[8:], work[:8]], axis=0), 120, 1)

    work = lax.fori_loop(0, NRHS // 8, eight, work)
    coeffs[...] = work

    @pl.loop(1, N_GX)
    def _(k):
        two_copy((gx + k) % N_GX, gx).wait_send()


def update_body(work, solution, residual, image, solution_next, residual_next, image_out):
    step = work[:, :NRHS].T
    solution_next[...] = solution[...] + dot(step, residual[...], precision=FULL)
    residual_next[...] = residual[...] - dot(step, image[...], precision=FULL)
    image_out[...] = image[...]


def shards(points, solution, residual, near_leaves, node_skeleton, upper_skeleton, far_nodes):
    vmem, hbm = (pl.BlockSpec(memory_space=m) for m in (pltpu.VMEM, pltpu.HBM))
    dma = pltpu.SemaphoreType.DMA
    residual_t = residual.T
    image_t, work = pl.pallas_call(
        kernel_body,
        out_shape=(
            jax.ShapeDtypeStruct((NRHS, CPD), F32),
            jax.ShapeDtypeStruct((NRHS, 128), F32),
        ),
        in_specs=[hbm] * 6,
        out_specs=(vmem, vmem),
        scratch_shapes=[
            pltpu.VMEM((D, CPD), BF16),
            pltpu.VMEM((NRHS, CPD), F32),
            pltpu.SMEM((2, NEAR), jnp.int32),
            pltpu.VMEM((1, RANK), jnp.int32),
            pltpu.VMEM((FIRST, RANK), jnp.int32),
            pltpu.SMEM((2, FAR), jnp.int32),
            pltpu.VMEM((NODES, PAY, RANK), BF16),
            pltpu.VMEM((2, LEAF_ROWS, LEAF), BF16),
            pltpu.VMEM((2, AUG, LEAF), BF16),
            pltpu.VMEM((2, LEAF, 128), BF16),
            pltpu.VMEM((N_GY, 16, 128), BF16),
            pltpu.VMEM((N_GY, LEAF_ROWS, LEAF), BF16),
            pltpu.VMEM((N_GY, LEAF_ROWS, LEAF), BF16),
            pltpu.VMEM((2, LEAF, NRHS), F32),
            pltpu.VMEM((2, LEAF, NRHS), F32),
            pltpu.VMEM((N_GY, 16, 128), F32),
            pltpu.VMEM((N_GX, 16, 128), F32),
            dma((6,)),
            dma((N_GY,)), dma((N_GY,)), dma((N_GY,)), dma((N_GY,)), dma((N_GY,)), dma((N_GY,)),
            dma((2, 2)), dma((2, 2)), dma((2,)), dma((2,)), dma((2,)), dma((2,)), dma((N_Y, 5)), dma((N_Y, 5)),
            dma((N_GY,)), dma((N_GY,)), dma((N_GX,)), dma((N_GX,)),
        ],
        compiler_params=pltpu.CompilerParams(
            collective_id=0, has_side_effects=True, vmem_limit_bytes=60 * 2**20
        ),
    )(points.T, residual_t, near_leaves, node_skeleton, upper_skeleton, far_nodes)
    outs = pl.pallas_call(
        update_body,
        out_shape=(jax.ShapeDtypeStruct((NRHS, CPD), F32),) * 3,
        in_specs=[vmem] * 4,
        out_specs=(vmem,) * 3,
    )(work, solution.T, residual_t, image_t)
    return tuple(o.T for o in outs)


def solution(mesh):
    split = P(("gx", "gy"), None)
    return jax.shard_map(
        shards,
        mesh=mesh,
        in_specs=(split, split, split, split, split, P(), split),
        out_specs=(split, split, split),
        check_vma=False,
    )
```

```python
import math

import jax
import jax.numpy as jnp
from jax import lax
from jax.experimental import pallas as pl
from jax.experimental.pallas import tpu as pltpu
from jax.sharding import PartitionSpec as P

D = 64
NRHS = 32
LEAF = 512
RANK = 128
NEAR = 4
FAR = 16
CPD = 1024
N_GX = 8
N_GY = 16
N_Y = 4
NODES = 255
FIRST = 127
AUG = D + 16
SENT = D + NRHS
PAY = SENT + 16
LEAF_ROWS = D + NRHS
SCALE = math.log2(math.e) / D
FULL = lax.Precision.HIGHEST
F32, BF16 = jnp.float32, jnp.bfloat16
MESH = pl.DeviceIdType.MESH


def dot(a, b, contract=((1,), (0,)), precision=None):
    return lax.dot_general(a, b, (contract, ((), ())), precision=precision, preferred_element_type=F32)


def square_rows(wide):
    half = -0.5 * jnp.sum(wide * wide, axis=0, keepdims=True)
    high = half.astype(BF16).astype(F32)
    rest = half - high
    middle = rest.astype(BF16).astype(F32)
    low = rest - middle
    row = lax.broadcasted_iota(jnp.int32, (16, wide.shape[1]), 0)
    ones = jnp.where((row >= 4) & (row < 7), 1.0, 0.0)
    return jnp.where(row == 0, high, jnp.where(row == 1, middle, jnp.where(row == 2, low, ones)))


def turned(rows):
    return jnp.concatenate([pltpu.roll(rows[:8], 4, 0), rows[8:]], axis=0)


def kernel_body(
    points_in, residual_in, near_in, skeleton_in, upper_in, far_in,
    image, coeffs,
    points, residual, near, skeleton, upper, far,
    nodes, own, own_right, own_left, asked, stage, leaves, near_acc, far_acc, part1, part2,
    in_s, req_s, req_r, pay_s, pay_r, near_s, near_r, y_s, y_r, on_s, on_r, sib_s, sib_r, full_s, full_r,
    one_s, one_r, two_s, two_r,
):
    gx, gy = lax.axis_index("gx"), lax.axis_index("gy")
    y, core = gx // 2, gx % 2
    me = gx * N_GY + gy
    sibling = 2 * y + (1 - core)

    pairs = ((near_in, near), (skeleton_in, skeleton), (points_in, points), (residual_in, residual), (upper_in, upper), (far_in, far))
    loads = [pltpu.make_async_copy(a, b, in_s.at[i]) for i, (a, b) in enumerate(pairs)]
    for load in loads:
        load.start()

    barrier = pltpu.get_barrier_semaphore()

    @pl.loop(1, N_GY)
    def _(k):
        pl.semaphore_signal(barrier, inc=1, device_id=(gx, (gy + k) % N_GY), device_id_type=MESH)

    @pl.loop(1, N_GX)
    def _(k):
        pl.semaphore_signal(barrier, inc=1, device_id=((gx + k) % N_GX, gy), device_id_type=MESH)

    def copy(src, dst, send, recv, device):
        return pltpu.make_async_remote_copy(
            src_ref=src, dst_ref=dst, send_sem=send, recv_sem=recv, device_id=device, device_id_type=MESH
        )

    for load in loads[1:4]:
        load.wait()

    @pl.loop(0, 2)
    def _(leaf):
        at = pl.ds(pl.multiple_of(leaf * LEAF, LEAF), LEAF)
        own_right[leaf, 0:D] = points[:, at]
        own_right[leaf, D:AUG] = square_rows(points[:, at].astype(F32)).astype(BF16)

    place = lax.broadcasted_iota(jnp.int32, (CPD, RANK), 0)
    skel = dot(points[...], jnp.where(place == skeleton[...], 1.0, 0.0).astype(BF16))
    rows = square_rows(skel)
    left = jnp.concatenate([skel, turned(rows), jnp.zeros((48, RANK), F32)], axis=0).T.astype(BF16)
    weights = jnp.zeros((NRHS, RANK), F32)
    for leaf in range(2):
        tile = jnp.exp2(SCALE * dot(left[:, :AUG], own_right[leaf]))
        weights += dot(residual[:, pl.ds(leaf * LEAF, LEAF)], tile, ((1,), (1,)), FULL)
    mine = FIRST + me
    nodes[mine, 0:D] = skel.astype(BF16)
    nodes[mine, D:SENT] = (weights * (1.0 / math.sqrt(CPD))).astype(BF16)

    pl.semaphore_wait(barrier, N_GY - 1 + N_GX - 1)

    def req_copy(peer, slot):
        return copy(asked.at[gy], asked.at[slot], req_s.at[peer], req_r.at[slot], (gx, peer))

    def pay_copy(peer, slot):
        at = FIRST + gx * N_GY + slot
        return copy(nodes.at[mine, pl.ds(0, SENT)], nodes.at[at, pl.ds(0, SENT)], pay_s.at[peer], pay_r.at[slot], (gx, peer))

    def near_copy(peer, slot):
        return copy(stage.at[peer], leaves.at[slot], near_s.at[peer], near_r.at[slot], (gx, peer))

    @pl.loop(1, N_GY)
    def _(k):
        pay_copy((gy + k) % N_GY, gy).start()

    loads[0].wait()
    row = lax.broadcasted_iota(jnp.int32, (16, 128), 0)
    wanted = jnp.full((16, 128), -1, jnp.int32)
    for leaf in range(2):
        for n in range(NEAR):
            wanted = jnp.where(row == leaf * NEAR + n, near[leaf, n], wanted)
    asked[gy] = wanted.astype(F32).astype(BF16)

    @pl.loop(1, N_GY)
    def _(k):
        req_copy((gy + k) % N_GY, gy).start()

    @pl.loop(0, 2)
    def _(leaf):
        at = pl.ds(pl.multiple_of(leaf * LEAF, LEAF), LEAF)
        wide = own_right[leaf].astype(F32)
        both = jnp.concatenate([wide[:D], turned(wide[D:]), jnp.zeros((48, LEAF), F32)], axis=0)
        own_left[leaf] = both.T.astype(BF16)
        own[leaf, 0:D] = points[:, at]
        own[leaf, D:LEAF_ROWS] = residual[:, at].astype(BF16)

    for load in loads[4:]:
        load.wait()

    def tile_term(leaf, right, values):
        tile = jnp.exp2(SCALE * dot(own_left[leaf, :, :AUG], right)).astype(BF16)
        return dot(tile, values, ((1,), (1,)))

    @pl.loop(0, 2)
    def _(leaf):
        near_acc[leaf] = tile_term(leaf, own_right[leaf], own[leaf, D:LEAF_ROWS])

    @pl.loop(1, N_GY)
    def _(k):
        peer = (gy + k) % N_GY
        pay_copy(peer, peer).wait_recv()

    def half(row, h):
        return nodes.at[pl.ds(FIRST + row * N_GY + h * 8, 8), pl.ds(0, SENT)]

    def row_of(step, other=False):
        return 2 * ((y + step) % N_Y) + (1 - core if other else core)

    def y_copy(step, h, source):
        to = (row_of(step), gy)
        k = 0 if step == 1 else 1
        return copy(half(gx, h), half(row_of(source), h), y_s.at[k, h], y_r.at[k, h], to)

    def on_copy(step, source):
        h = k = 0 if step == 1 else 1
        return copy(half(row_of(-step), h), half(row_of(source), h), on_s.at[k], on_r.at[k], (row_of(step), gy))

    def sib_copy(h, other):
        return copy(half(row_of(2), h), half(row_of(2, other), h), sib_s.at[h], sib_r.at[h], (sibling, gy))

    for h in range(2):
        y_copy(1, h, 0).start()
        y_copy(-1, 1 - h, 0).start()

    this = (2 * me + 1).astype(F32)
    leaves[gy] = own[0]

    @pl.loop(1, N_GY)
    def _(k):
        peer = (gy + k) % N_GY
        req_copy(peer, peer).wait_recv()
        second = jnp.where(asked[peer].astype(F32) == this, 1.0, 0.0)
        second = jnp.max(second, axis=0, keepdims=True)
        second = jnp.concatenate([second] * 4, axis=1)
        for r in range(0, LEAF_ROWS, 32):
            at = pl.ds(r, 32)
            stage[peer, at] = jnp.where(
                jnp.broadcast_to(second, (32, LEAF)) > 0.5, own[1, at].astype(F32), own[0, at].astype(F32)
            ).astype(BF16)
        near_copy(peer, gy).start()

    def right_of(node):
        return jnp.concatenate([node[:D], node[SENT:]], axis=0)

    def build(first, count):
        done = []
        for i in range(count):
            u = first + i
            a, b = nodes[2 * u + 1], nodes[2 * u + 2]
            choice = jnp.broadcast_to(upper[pl.ds(u, 1), :], (AUG, RANK))
            lane = jnp.bitwise_and(choice, RANK - 1)
            from_a, from_b = (
                jnp.take_along_axis(right_of(x).astype(F32), lane, axis=1, mode="promise_in_bounds") for x in (a, b)
            )
            right = jnp.where(choice < RANK, from_a, from_b)
            left = jnp.concatenate([right[:D], turned(right[D:])], axis=0).astype(BF16)
            both = jnp.concatenate([a, b], axis=1)
            tile = jnp.exp2(SCALE * dot(left, right_of(both), ((0,), (0,)))).astype(BF16)
            sums = dot(both[D:], tile, ((1,), (1,)))
            weights = sums[:NRHS] / sums[NRHS + 4 : NRHS + 5]
            done.append(jnp.concatenate([right[:D], weights, right[D:]], axis=0).astype(BF16))
        for i, node in enumerate(done):
            nodes[first + i] = node

    def build_row(row):
        for h in range(2):
            first = FIRST + row * N_GY + h * 8
            wide = jnp.concatenate([nodes[first + i, 0:D].astype(F32) for i in range(8)], axis=1)
            rows = square_rows(wide).astype(BF16)
            for i in range(8):
                nodes[first + i, SENT:PAY] = rows[:, i * RANK : (i + 1) * RANK]
        build(63 + row * 8, 8)
        build(31 + row * 4, 4)
        build(15 + row * 2, 2)
        build(7 + row, 1)

    def near_tile(n):
        leaf, pair = n // (NEAR // 2), n % (NEAR // 2)
        got = [leaves[(near[leaf, 2 * pair + i] // 2) % N_GY] for i in range(2)]
        got = jnp.concatenate(got, axis=1)
        right = jnp.concatenate([got[:D], square_rows(got[:D].astype(F32)).astype(BF16)], axis=0)
        near_acc[leaf] = near_acc[leaf] + tile_term(leaf, right, got[D:])

    def run(row, level):
        return nodes.at[pl.ds(2**level - 1 + row * (2**level // N_GX), 2**level // N_GX)]

    def full_copy(step, level, other):
        at = (y + step) % N_Y
        send, recv = full_s.at[at, level - 3], full_r.at[at, level - 3]
        return copy(run(row_of(step), level), run(row_of(step, other), level), send, recv, (sibling, gy))

    @pl.loop(0, N_Y + 1)
    def _(i):
        @pl.when(i == 1)
        def _():
            for step in (1, -1):
                h = 0 if step == 1 else 1
                y_copy(step, h, -step).wait_recv()
                on_copy(step, -step).start()
            y_copy(-1, 0, 1).wait_recv()

        @pl.when(i == 2)
        def _():
            y_copy(1, 1, -1).wait_recv()

        @pl.when(i == 3)
        def _():
            for step in (1, -1):
                on_copy(step, 2).wait_recv()
                sib_copy(0 if step == 1 else 1, False).start()

        @pl.when(i == 4)
        def _():
            for h in range(2):
                sib_copy(h, True).wait_recv()

        turn = i - i // N_Y
        away = turn + turn // 2 - 2 * (turn // 3)
        build_row(2 * ((y + away) % N_Y) + (core + i // N_Y) % 2)

        @pl.when(i < 3)
        def _():
            for level in range(7, 2, -1):
                full_copy(away, level, False).start()

    for step in (0, 1, -1):
        for level in range(7, 2, -1):
            full_copy(step, level, True).wait_recv()

    build(3, 4)
    build(1, 2)
    build(0, 1)

    far_acc[...] = jnp.zeros_like(far_acc)

    @pl.loop(0, FAR // 4)
    def _(n):
        leaf, group = n // (FAR // 8), n % (FAR // 8)
        got = jnp.concatenate([nodes[far[leaf, 8 * group + i]] for i in range(8)], axis=1)
        far_acc[leaf] = far_acc[leaf] + tile_term(leaf, right_of(got), got[D:SENT])

    @pl.loop(1, N_GY)
    def _(k):
        peer = (gy + k) % N_GY
        near_copy(peer, peer).wait_recv()

    pl.loop(0, NEAR)(near_tile)

    for leaf in range(2):
        at = pl.ds(leaf * LEAF, LEAF)
        terms = near_acc[leaf] * (1.0 / math.sqrt(LEAF)) + far_acc[leaf] * (1.0 / RANK)
        image[:, at] = residual[:, at] + terms.T

    both = jnp.concatenate([image[...], residual[...]], axis=0)
    gram = dot(image[...], both, ((1,), (1,)), FULL)
    part1[gy] = jnp.concatenate([gram[:16], gram[16:]], axis=1)

    def one_copy(peer, slot):
        return copy(part1.at[gy], part1.at[slot], one_s.at[peer], one_r.at[slot], (gx, peer))

    def two_copy(peer, slot):
        return copy(part2.at[gx], part2.at[slot], two_s.at[peer], two_r.at[slot], (peer, gy))

    @pl.loop(1, N_GY)
    def _(k):
        one_copy((gy + k) % N_GY, gy).start()

    @pl.loop(1, N_GY)
    def _(k):
        peer = (gy + k) % N_GY
        req_copy(peer, gy).wait_send()
        pay_copy(peer, gy).wait_send()
        near_copy(peer, gy).wait_send()

    for step in (1, -1):
        for h in range(2):
            y_copy(step, h, 0).wait_send()
        on_copy(step, -step).wait_send()
    for h in range(2):
        sib_copy(h, False).wait_send()

    @pl.loop(0, 3)
    def _(i):
        for level in range(7, 2, -1):
            full_copy(i - 1, level, False).wait_send()

    @pl.loop(1, N_GY)
    def _(k):
        peer = (gy + k) % N_GY
        one_copy(peer, peer).wait_recv()

    total = part1[0]
    for k in range(1, N_GY):
        total += part1[k]
    part2[gx] = total

    @pl.loop(1, N_GX)
    def _(k):
        two_copy((gx + k) % N_GX, gx).start()

    @pl.loop(1, N_GY)
    def _(k):
        one_copy((gy + k) % N_GY, gy).wait_send()

    @pl.loop(1, N_GX)
    def _(k):
        peer = (gx + k) % N_GX
        two_copy(peer, peer).wait_recv()

    total = part2[0]
    for k in range(1, N_GX):
        total += part2[k]

    work = jnp.concatenate([total, pltpu.roll(total, 64, 1)], axis=0)

    def eight(_, work):
        columns = [jnp.broadcast_to(work[:, i : i + 1], (NRHS, 128)) for i in range(8)]
        block = [[columns[j][i : i + 1] for j in range(8)] for i in range(8)]
        rows = [work[i : i + 1] for i in range(8)]
        for i in range(8):
            inverse = 1.0 / block[i][i]
            rows[i] = rows[i] * inverse
            for j in range(i + 1, 8):
                block[i][j] = block[i][j] * inverse
            for r in range(i + 1, 8):
                for j in range(i + 1, 8):
                    block[r][j] = block[r][j] - block[r][i] * block[i][j]
                rows[r] = rows[r] - block[r][i] * rows[i]
        for i in range(7, 0, -1):
            for r in range(i):
                rows[r] = rows[r] - block[r][i] * rows[i]
        rest = work
        for i in range(8):
            rest = rest - columns[i] * rows[i]
        return pltpu.roll(jnp.concatenate([rest[8:], *rows], axis=0), 120, 1)

    work = lax.fori_loop(0, NRHS // 8, eight, work)
    coeffs[...] = work

    @pl.loop(1, N_GX)
    def _(k):
        two_copy((gx + k) % N_GX, gx).wait_send()


def update_body(work, solution, residual, image, solution_next, residual_next, image_out):
    step = work[:, :NRHS].T
    solution_next[...] = solution[...] + dot(step, residual[...], precision=FULL)
    residual_next[...] = residual[...] - dot(step, image[...], precision=FULL)
    image_out[...] = image[...]


def shards(points, solution, residual, near_leaves, node_skeleton, upper_skeleton, far_nodes):
    vmem, hbm = (pl.BlockSpec(memory_space=m) for m in (pltpu.VMEM, pltpu.HBM))
    dma = pltpu.SemaphoreType.DMA
    residual_t = residual.T
    image_t, work = pl.pallas_call(
        kernel_body,
        out_shape=(
            jax.ShapeDtypeStruct((NRHS, CPD), F32),
            jax.ShapeDtypeStruct((NRHS, 128), F32),
        ),
        in_specs=[hbm] * 6,
        out_specs=(vmem, vmem),
        scratch_shapes=[
            pltpu.VMEM((D, CPD), BF16),
            pltpu.VMEM((NRHS, CPD), F32),
            pltpu.SMEM((2, NEAR), jnp.int32),
            pltpu.VMEM((1, RANK), jnp.int32),
            pltpu.VMEM((FIRST, RANK), jnp.int32),
            pltpu.SMEM((2, FAR), jnp.int32),
            pltpu.VMEM((NODES, PAY, RANK), BF16),
            pltpu.VMEM((2, LEAF_ROWS, LEAF), BF16),
            pltpu.VMEM((2, AUG, LEAF), BF16),
            pltpu.VMEM((2, LEAF, 128), BF16),
            pltpu.VMEM((N_GY, 16, 128), BF16),
            pltpu.VMEM((N_GY, LEAF_ROWS, LEAF), BF16),
            pltpu.VMEM((N_GY, LEAF_ROWS, LEAF), BF16),
            pltpu.VMEM((2, LEAF, NRHS), F32),
            pltpu.VMEM((2, LEAF, NRHS), F32),
            pltpu.VMEM((N_GY, 16, 128), F32),
            pltpu.VMEM((N_GX, 16, 128), F32),
            dma((6,)),
            dma((N_GY,)), dma((N_GY,)), dma((N_GY,)), dma((N_GY,)), dma((N_GY,)), dma((N_GY,)),
            dma((2, 2)), dma((2, 2)), dma((2,)), dma((2,)), dma((2,)), dma((2,)), dma((N_Y, 5)), dma((N_Y, 5)),
            dma((N_GY,)), dma((N_GY,)), dma((N_GX,)), dma((N_GX,)),
        ],
        compiler_params=pltpu.CompilerParams(
            collective_id=0, has_side_effects=True, vmem_limit_bytes=60 * 2**20
        ),
    )(points.T, residual_t, near_leaves, node_skeleton, upper_skeleton, far_nodes)
    outs = pl.pallas_call(
        update_body,
        out_shape=(jax.ShapeDtypeStruct((NRHS, CPD), F32),) * 3,
        in_specs=[vmem] * 4,
        out_specs=(vmem,) * 3,
    )(work, solution.T, residual_t, image_t)
    return tuple(o.T for o in outs)


def solution(mesh):
    split = P(("gx", "gy"), None)
    return jax.shard_map(
        shards,
        mesh=mesh,
        in_specs=(split, split, split, split, split, P(), split),
        out_specs=(split, split, split),
        check_vma=False,
    )
```

```python
import math

import jax
import jax.numpy as jnp
from jax import lax
from jax.experimental import pallas as pl
from jax.experimental.pallas import tpu as pltpu
from jax.sharding import PartitionSpec as P

D = 64
NRHS = 32
LEAF = 512
RANK = 128
NEAR = 4
FAR = 16
CPD = 1024
N_GX = 8
N_GY = 16
N_Y = 4
NODES = 255
FIRST = 127
AUG = D + 16
SENT = D + NRHS
PAY = SENT + 16
LEAF_ROWS = D + NRHS
SCALE = math.log2(math.e) / D
FULL = lax.Precision.HIGHEST
F32, BF16 = jnp.float32, jnp.bfloat16
MESH = pl.DeviceIdType.MESH


def dot(a, b, contract=((1,), (0,)), precision=None):
    return lax.dot_general(a, b, (contract, ((), ())), precision=precision, preferred_element_type=F32)


def square_rows(wide):
    half = -0.5 * jnp.sum(wide * wide, axis=0, keepdims=True)
    high = half.astype(BF16).astype(F32)
    rest = half - high
    middle = rest.astype(BF16).astype(F32)
    low = rest - middle
    row = lax.broadcasted_iota(jnp.int32, (16, wide.shape[1]), 0)
    ones = jnp.where((row >= 4) & (row < 7), 1.0, 0.0)
    return jnp.where(row == 0, high, jnp.where(row == 1, middle, jnp.where(row == 2, low, ones)))


def turned(rows):
    return jnp.concatenate([pltpu.roll(rows[:8], 4, 0), rows[8:]], axis=0)


def kernel_body(
    points_in, residual_in, near_in, skeleton_in, upper_in, far_in,
    image, coeffs,
    points, residual, near, skeleton, upper, far,
    nodes, own, own_right, own_left, asked, stage, leaves, near_acc, far_acc, part1, part2,
    in_s, req_s, req_r, pay_s, pay_r, near_s, near_r, y_s, y_r, on_s, on_r, sib_s, sib_r, full_s, full_r,
    one_s, one_r, two_s, two_r,
):
    gx, gy = lax.axis_index("gx"), lax.axis_index("gy")
    y, core = gx // 2, gx % 2
    me = gx * N_GY + gy
    sibling = 2 * y + (1 - core)

    pairs = ((near_in, near), (skeleton_in, skeleton), (points_in, points), (residual_in, residual), (upper_in, upper), (far_in, far))
    loads = [pltpu.make_async_copy(a, b, in_s.at[i]) for i, (a, b) in enumerate(pairs)]
    for load in loads:
        load.start()

    barrier = pltpu.get_barrier_semaphore()

    @pl.loop(1, N_GY)
    def _(k):
        pl.semaphore_signal(barrier, inc=1, device_id=(gx, (gy + k) % N_GY), device_id_type=MESH)

    @pl.loop(1, N_GX)
    def _(k):
        pl.semaphore_signal(barrier, inc=1, device_id=((gx + k) % N_GX, gy), device_id_type=MESH)

    def copy(src, dst, send, recv, device):
        return pltpu.make_async_remote_copy(
            src_ref=src, dst_ref=dst, send_sem=send, recv_sem=recv, device_id=device, device_id_type=MESH
        )

    for load in loads[1:4]:
        load.wait()

    @pl.loop(0, 2)
    def _(leaf):
        at = pl.ds(pl.multiple_of(leaf * LEAF, LEAF), LEAF)
        own_right[leaf, 0:D] = points[:, at]
        own_right[leaf, D:AUG] = square_rows(points[:, at].astype(F32)).astype(BF16)

    place = lax.broadcasted_iota(jnp.int32, (CPD, RANK), 0)
    skel = dot(points[...], jnp.where(place == skeleton[...], 1.0, 0.0).astype(BF16))
    rows = square_rows(skel)
    left = jnp.concatenate([skel, turned(rows), jnp.zeros((48, RANK), F32)], axis=0).T.astype(BF16)
    weights = jnp.zeros((NRHS, RANK), F32)
    for leaf in range(2):
        tile = jnp.exp2(SCALE * dot(left[:, :AUG], own_right[leaf]))
        weights += dot(residual[:, pl.ds(leaf * LEAF, LEAF)], tile, ((1,), (1,)), FULL)
    mine = FIRST + me
    nodes[mine, 0:D] = skel.astype(BF16)
    nodes[mine, D:SENT] = (weights * (1.0 / math.sqrt(CPD))).astype(BF16)

    pl.semaphore_wait(barrier, N_GY - 1 + N_GX - 1)

    def req_copy(peer, slot):
        return copy(asked.at[gy], asked.at[slot], req_s.at[peer], req_r.at[slot], (gx, peer))

    def pay_copy(peer, slot):
        at = FIRST + gx * N_GY + slot
        return copy(nodes.at[mine, pl.ds(0, SENT)], nodes.at[at, pl.ds(0, SENT)], pay_s.at[0], pay_r.at[0], (gx, peer))

    def all_pay():
        part = nodes.at[pl.ds(FIRST + gx * N_GY, N_GY - 1), pl.ds(0, SENT)]
        return copy(part, part, pay_s.at[0], pay_r.at[0], (gx, (gy + 1) % N_GY))

    def near_copy(peer, slot):
        return copy(stage.at[peer], leaves.at[slot], near_s.at[peer], near_r.at[slot], (gx, peer))

    @pl.loop(1, N_GY)
    def _(k):
        pay_copy((gy + k) % N_GY, gy).start()

    loads[0].wait()
    row = lax.broadcasted_iota(jnp.int32, (16, 128), 0)
    wanted = jnp.full((16, 128), -1, jnp.int32)
    for leaf in range(2):
        for n in range(NEAR):
            wanted = jnp.where(row == leaf * NEAR + n, near[leaf, n], wanted)
    asked[gy] = wanted.astype(F32).astype(BF16)

    @pl.loop(1, N_GY)
    def _(k):
        req_copy((gy + k) % N_GY, gy).start()

    @pl.loop(0, 2)
    def _(leaf):
        at = pl.ds(pl.multiple_of(leaf * LEAF, LEAF), LEAF)
        wide = own_right[leaf].astype(F32)
        both = jnp.concatenate([wide[:D], turned(wide[D:]), jnp.zeros((48, LEAF), F32)], axis=0)
        own_left[leaf] = both.T.astype(BF16)
        own[leaf, 0:D] = points[:, at]
        own[leaf, D:LEAF_ROWS] = residual[:, at].astype(BF16)

    for load in loads[4:]:
        load.wait()

    def tile_term(leaf, right, values):
        tile = jnp.exp2(SCALE * dot(own_left[leaf, :, :AUG], right)).astype(BF16)
        return dot(tile, values, ((1,), (1,)))

    @pl.loop(0, 2)
    def _(leaf):
        near_acc[leaf] = tile_term(leaf, own_right[leaf], own[leaf, D:LEAF_ROWS])

    all_pay().wait_recv()

    def half(row, h):
        return nodes.at[pl.ds(FIRST + row * N_GY + h * 8, 8), pl.ds(0, SENT)]

    def row_of(step, other=False):
        return 2 * ((y + step) % N_Y) + (1 - core if other else core)

    def y_copy(step, h, source):
        to = (row_of(step), gy)
        k = 0 if step == 1 else 1
        return copy(half(gx, h), half(row_of(source), h), y_s.at[k, h], y_r.at[k, h], to)

    def on_copy(step, source):
        h = k = 0 if step == 1 else 1
        return copy(half(row_of(-step), h), half(row_of(source), h), on_s.at[k], on_r.at[k], (row_of(step), gy))

    def sib_copy(h, other):
        return copy(half(row_of(2), h), half(row_of(2, other), h), sib_s.at[h], sib_r.at[h], (sibling, gy))

    for h in range(2):
        y_copy(1, h, 0).start()
        y_copy(-1, 1 - h, 0).start()

    this = (2 * me + 1).astype(F32)
    leaves[gy] = own[0]

    @pl.loop(1, N_GY)
    def _(k):
        peer = (gy + k) % N_GY
        req_copy(peer, peer).wait_recv()
        second = jnp.where(asked[peer].astype(F32) == this, 1.0, 0.0)
        second = jnp.max(second, axis=0, keepdims=True)
        second = jnp.concatenate([second] * 4, axis=1)
        for r in range(0, LEAF_ROWS, 32):
            at = pl.ds(r, 32)
            stage[peer, at] = jnp.where(
                jnp.broadcast_to(second, (32, LEAF)) > 0.5, own[1, at].astype(F32), own[0, at].astype(F32)
            ).astype(BF16)
        near_copy(peer, gy).start()

    def right_of(node):
        return jnp.concatenate([node[:D], node[SENT:]], axis=0)

    def build(first, count):
        done = []
        for i in range(count):
            u = first + i
            a, b = nodes[2 * u + 1], nodes[2 * u + 2]
            choice = jnp.broadcast_to(upper[pl.ds(u, 1), :], (AUG, RANK))
            lane = jnp.bitwise_and(choice, RANK - 1)
            from_a, from_b = (
                jnp.take_along_axis(right_of(x).astype(F32), lane, axis=1, mode="promise_in_bounds") for x in (a, b)
            )
            right = jnp.where(choice < RANK, from_a, from_b)
            left = jnp.concatenate([right[:D], turned(right[D:])], axis=0).astype(BF16)
            both = jnp.concatenate([a, b], axis=1)
            tile = jnp.exp2(SCALE * dot(left, right_of(both), ((0,), (0,)))).astype(BF16)
            sums = dot(both[D:], tile, ((1,), (1,)))
            weights = sums[:NRHS] / sums[NRHS + 4 : NRHS + 5]
            done.append(jnp.concatenate([right[:D], weights, right[D:]], axis=0).astype(BF16))
        for i, node in enumerate(done):
            nodes[first + i] = node

    def build_row(row):
        for h in range(2):
            first = FIRST + row * N_GY + h * 8
            wide = jnp.concatenate([nodes[first + i, 0:D].astype(F32) for i in range(8)], axis=1)
            rows = square_rows(wide).astype(BF16)
            for i in range(8):
                nodes[first + i, SENT:PAY] = rows[:, i * RANK : (i + 1) * RANK]
        build(63 + row * 8, 8)
        build(31 + row * 4, 4)
        build(15 + row * 2, 2)
        build(7 + row, 1)

    def near_tile(n):
        leaf, pair = n // (NEAR // 2), n % (NEAR // 2)
        got = [leaves[(near[leaf, 2 * pair + i] // 2) % N_GY] for i in range(2)]
        got = jnp.concatenate(got, axis=1)
        right = jnp.concatenate([got[:D], square_rows(got[:D].astype(F32)).astype(BF16)], axis=0)
        near_acc[leaf] = near_acc[leaf] + tile_term(leaf, right, got[D:])

    def run(row, level):
        return nodes.at[pl.ds(2**level - 1 + row * (2**level // N_GX), 2**level // N_GX)]

    def full_copy(step, level, other):
        at = (y + step) % N_Y
        send, recv = full_s.at[at, level - 3], full_r.at[at, level - 3]
        return copy(run(row_of(step), level), run(row_of(step, other), level), send, recv, (sibling, gy))

    @pl.loop(0, N_Y + 1)
    def _(i):
        @pl.when(i == 1)
        def _():
            for step in (1, -1):
                h = 0 if step == 1 else 1
                y_copy(step, h, -step).wait_recv()
                on_copy(step, -step).start()
            y_copy(-1, 0, 1).wait_recv()

        @pl.when(i == 2)
        def _():
            y_copy(1, 1, -1).wait_recv()

        @pl.when(i == 3)
        def _():
            for step in (1, -1):
                on_copy(step, 2).wait_recv()
                sib_copy(0 if step == 1 else 1, False).start()

        @pl.when(i == 4)
        def _():
            for h in range(2):
                sib_copy(h, True).wait_recv()

        turn = i - i // N_Y
        away = turn + turn // 2 - 2 * (turn // 3)
        build_row(2 * ((y + away) % N_Y) + (core + i // N_Y) % 2)

        @pl.when(i < 3)
        def _():
            for level in range(7, 2, -1):
                full_copy(away, level, False).start()

    for step in (0, 1, -1):
        for level in range(7, 2, -1):
            full_copy(step, level, True).wait_recv()

    build(3, 4)
    build(1, 2)
    build(0, 1)

    far_acc[...] = jnp.zeros_like(far_acc)

    @pl.loop(0, FAR // 4)
    def _(n):
        leaf, group = n // (FAR // 8), n % (FAR // 8)
        got = jnp.concatenate([nodes[far[leaf, 8 * group + i]] for i in range(8)], axis=1)
        far_acc[leaf] = far_acc[leaf] + tile_term(leaf, right_of(got), got[D:SENT])

    @pl.loop(1, N_GY)
    def _(k):
        peer = (gy + k) % N_GY
        near_copy(peer, peer).wait_recv()

    pl.loop(0, NEAR)(near_tile)

    for leaf in range(2):
        at = pl.ds(leaf * LEAF, LEAF)
        terms = near_acc[leaf] * (1.0 / math.sqrt(LEAF)) + far_acc[leaf] * (1.0 / RANK)
        image[:, at] = residual[:, at] + terms.T

    both = jnp.concatenate([image[...], residual[...]], axis=0)
    gram = dot(image[...], both, ((1,), (1,)), FULL)
    part1[gy] = jnp.concatenate([gram[:16], gram[16:]], axis=1)

    def one_copy(peer, slot):
        return copy(part1.at[gy], part1.at[slot], one_s.at[0], one_r.at[0], (gx, peer))

    def all_one():
        part = part1.at[pl.ds(0, N_GY - 1)]
        return copy(part, part, one_s.at[0], one_r.at[0], (gx, (gy + 1) % N_GY))

    def all_two():
        part = part2.at[pl.ds(0, N_GX - 1)]
        return copy(part, part, two_s.at[0], two_r.at[0], ((gx + 1) % N_GX, gy))

    def two_copy(peer, slot):
        return copy(part2.at[gx], part2.at[slot], two_s.at[0], two_r.at[0], (peer, gy))

    @pl.loop(1, N_GY)
    def _(k):
        one_copy((gy + k) % N_GY, gy).start()

    @pl.loop(1, N_GY)
    def _(k):
        peer = (gy + k) % N_GY
        req_copy(peer, gy).wait_send()
        near_copy(peer, gy).wait_send()

    all_pay().wait_send()
    for step in (1, -1):
        for h in range(2):
            y_copy(step, h, 0).wait_send()
        on_copy(step, -step).wait_send()
    for h in range(2):
        sib_copy(h, False).wait_send()

    @pl.loop(0, 3)
    def _(i):
        for level in range(7, 2, -1):
            full_copy(i - 1, level, False).wait_send()

    all_one().wait_recv()

    total = part1[0]
    for k in range(1, N_GY):
        total += part1[k]
    part2[gx] = total

    @pl.loop(1, N_GX)
    def _(k):
        two_copy((gx + k) % N_GX, gx).start()

    all_one().wait_send()

    all_two().wait_recv()

    total = part2[0]
    for k in range(1, N_GX):
        total += part2[k]

    work = jnp.concatenate([total, pltpu.roll(total, 64, 1)], axis=0)

    def eight(_, work):
        columns = [jnp.broadcast_to(work[:, i : i + 1], (NRHS, 128)) for i in range(8)]
        block = [[columns[j][i : i + 1] for j in range(8)] for i in range(8)]
        rows = [work[i : i + 1] for i in range(8)]
        for i in range(8):
            inverse = 1.0 / block[i][i]
            rows[i] = rows[i] * inverse
            for j in range(i + 1, 8):
                block[i][j] = block[i][j] * inverse
            for r in range(i + 1, 8):
                for j in range(i + 1, 8):
                    block[r][j] = block[r][j] - block[r][i] * block[i][j]
                rows[r] = rows[r] - block[r][i] * rows[i]
        for i in range(7, 0, -1):
            for r in range(i):
                rows[r] = rows[r] - block[r][i] * rows[i]
        rest = work
        for i in range(8):
            rest = rest - columns[i] * rows[i]
        return pltpu.roll(jnp.concatenate([rest[8:], *rows], axis=0), 120, 1)

    work = lax.fori_loop(0, NRHS // 8, eight, work)
    coeffs[...] = work

    all_two().wait_send()


def update_body(work, solution, residual, image, solution_next, residual_next, image_out):
    step = work[:, :NRHS].T
    solution_next[...] = solution[...] + dot(step, residual[...], precision=FULL)
    residual_next[...] = residual[...] - dot(step, image[...], precision=FULL)
    image_out[...] = image[...]


def shards(points, solution, residual, near_leaves, node_skeleton, upper_skeleton, far_nodes):
    vmem, hbm = (pl.BlockSpec(memory_space=m) for m in (pltpu.VMEM, pltpu.HBM))
    dma = pltpu.SemaphoreType.DMA
    residual_t = residual.T
    image_t, work = pl.pallas_call(
        kernel_body,
        out_shape=(
            jax.ShapeDtypeStruct((NRHS, CPD), F32),
            jax.ShapeDtypeStruct((NRHS, 128), F32),
        ),
        in_specs=[hbm] * 6,
        out_specs=(vmem, vmem),
        scratch_shapes=[
            pltpu.VMEM((D, CPD), BF16),
            pltpu.VMEM((NRHS, CPD), F32),
            pltpu.SMEM((2, NEAR), jnp.int32),
            pltpu.VMEM((1, RANK), jnp.int32),
            pltpu.VMEM((FIRST, RANK), jnp.int32),
            pltpu.SMEM((2, FAR), jnp.int32),
            pltpu.VMEM((NODES, PAY, RANK), BF16),
            pltpu.VMEM((2, LEAF_ROWS, LEAF), BF16),
            pltpu.VMEM((2, AUG, LEAF), BF16),
            pltpu.VMEM((2, LEAF, 128), BF16),
            pltpu.VMEM((N_GY, 16, 128), BF16),
            pltpu.VMEM((N_GY, LEAF_ROWS, LEAF), BF16),
            pltpu.VMEM((N_GY, LEAF_ROWS, LEAF), BF16),
            pltpu.VMEM((2, LEAF, NRHS), F32),
            pltpu.VMEM((2, LEAF, NRHS), F32),
            pltpu.VMEM((N_GY, 16, 128), F32),
            pltpu.VMEM((N_GX, 16, 128), F32),
            dma((6,)),
            dma((N_GY,)), dma((N_GY,)), dma((1,)), dma((1,)), dma((N_GY,)), dma((N_GY,)),
            dma((2, 2)), dma((2, 2)), dma((2,)), dma((2,)), dma((2,)), dma((2,)), dma((N_Y, 5)), dma((N_Y, 5)),
            dma((1,)), dma((1,)), dma((1,)), dma((1,)),
        ],
        compiler_params=pltpu.CompilerParams(
            collective_id=0, has_side_effects=True, vmem_limit_bytes=60 * 2**20
        ),
    )(points.T, residual_t, near_leaves, node_skeleton, upper_skeleton, far_nodes)
    outs = pl.pallas_call(
        update_body,
        out_shape=(jax.ShapeDtypeStruct((NRHS, CPD), F32),) * 3,
        in_specs=[vmem] * 4,
        out_specs=(vmem,) * 3,
    )(work, solution.T, residual_t, image_t)
    return tuple(o.T for o in outs)


def solution(mesh):
    split = P(("gx", "gy"), None)
    return jax.shard_map(
        shards,
        mesh=mesh,
        in_specs=(split, split, split, split, split, P(), split),
        out_specs=(split, split, split),
        check_vma=False,
    )
```

```python
import math

import jax
import jax.numpy as jnp
from jax import lax
from jax.experimental import pallas as pl
from jax.experimental.pallas import tpu as pltpu
from jax.sharding import PartitionSpec as P

D = 64
NRHS = 32
LEAF = 512
RANK = 128
NEAR = 4
FAR = 16
CPD = 1024
N_GX = 8
N_GY = 16
N_Y = 4
NODES = 255
FIRST = 127
AUG = D + 16
SENT = D + NRHS
PAY = SENT + 16
LEAF_ROWS = D + NRHS
SCALE = math.log2(math.e) / D
FULL = lax.Precision.HIGHEST
F32, BF16 = jnp.float32, jnp.bfloat16
MESH = pl.DeviceIdType.MESH


def dot(a, b, contract=((1,), (0,)), precision=None):
    return lax.dot_general(a, b, (contract, ((), ())), precision=precision, preferred_element_type=F32)


def square_rows(wide):
    half = -0.5 * jnp.sum(wide * wide, axis=0, keepdims=True)
    high = half.astype(BF16).astype(F32)
    rest = half - high
    middle = rest.astype(BF16).astype(F32)
    low = rest - middle
    row = lax.broadcasted_iota(jnp.int32, (16, wide.shape[1]), 0)
    ones = jnp.where((row >= 4) & (row < 7), 1.0, 0.0)
    return jnp.where(row == 0, high, jnp.where(row == 1, middle, jnp.where(row == 2, low, ones)))


def turned(rows):
    return jnp.concatenate([pltpu.roll(rows[:8], 4, 0), rows[8:]], axis=0)


def kernel_body(
    points_in, residual_in, near_in, skeleton_in, upper_in, far_in,
    image, coeffs,
    points, residual, near, skeleton, upper, far,
    nodes, own, own_right, own_left, asked, stage, leaves, near_acc, far_acc, part1, part2,
    in_s, req_s, req_r, pay_s, pay_r, near_s, near_r, y_s, y_r, on_s, on_r, sib_s, sib_r, full_s, full_r,
    one_s, one_r, two_s, two_r,
):
    gx, gy = lax.axis_index("gx"), lax.axis_index("gy")
    y, core = gx // 2, gx % 2
    me = gx * N_GY + gy
    sibling = 2 * y + (1 - core)

    pairs = ((near_in, near), (skeleton_in, skeleton), (points_in, points), (residual_in, residual), (upper_in, upper), (far_in, far))
    loads = [pltpu.make_async_copy(a, b, in_s.at[i]) for i, (a, b) in enumerate(pairs)]
    for load in loads:
        load.start()

    barrier = pltpu.get_barrier_semaphore()

    @pl.loop(1, N_GY)
    def _(k):
        pl.semaphore_signal(barrier, inc=1, device_id=(gx, (gy + k) % N_GY), device_id_type=MESH)

    @pl.loop(1, N_GX)
    def _(k):
        pl.semaphore_signal(barrier, inc=1, device_id=((gx + k) % N_GX, gy), device_id_type=MESH)

    def copy(src, dst, send, recv, device):
        return pltpu.make_async_remote_copy(
            src_ref=src, dst_ref=dst, send_sem=send, recv_sem=recv, device_id=device, device_id_type=MESH
        )

    for load in loads[1:4]:
        load.wait()

    @pl.loop(0, 2)
    def _(leaf):
        at = pl.ds(pl.multiple_of(leaf * LEAF, LEAF), LEAF)
        own_right[leaf, 0:D] = points[:, at]
        own_right[leaf, D:AUG] = square_rows(points[:, at].astype(F32)).astype(BF16)

    place = lax.broadcasted_iota(jnp.int32, (CPD, RANK), 0)
    skel = dot(points[...], jnp.where(place == skeleton[...], 1.0, 0.0).astype(BF16))
    rows = square_rows(skel)
    left = jnp.concatenate([skel, turned(rows), jnp.zeros((48, RANK), F32)], axis=0).T.astype(BF16)
    weights = jnp.zeros((NRHS, RANK), F32)
    for leaf in range(2):
        tile = jnp.exp2(SCALE * dot(left[:, :AUG], own_right[leaf]))
        weights += dot(residual[:, pl.ds(leaf * LEAF, LEAF)], tile, ((1,), (1,)), FULL)
    mine = FIRST + me
    nodes[mine, 0:D] = skel.astype(BF16)
    nodes[mine, D:SENT] = (weights * (1.0 / math.sqrt(CPD))).astype(BF16)

    pl.semaphore_wait(barrier, N_GY - 1 + N_GX - 1)

    def req_copy(peer, slot):
        return copy(asked.at[gy], asked.at[slot], req_s.at[peer], req_r.at[slot], (gx, peer))

    def pay_copy(peer, slot):
        at = FIRST + gx * N_GY + slot
        return copy(nodes.at[mine, pl.ds(0, SENT)], nodes.at[at, pl.ds(0, SENT)], pay_s.at[0], pay_r.at[0], (gx, peer))

    def all_pay():
        part = nodes.at[pl.ds(FIRST + gx * N_GY, N_GY - 1), pl.ds(0, SENT)]
        return copy(part, part, pay_s.at[0], pay_r.at[0], (gx, (gy + 1) % N_GY))

    def near_copy(peer, slot):
        return copy(stage.at[peer], leaves.at[slot], near_s.at[0], near_r.at[0], (gx, peer))

    def all_near():
        src, dst = stage.at[pl.ds(0, N_GY - 1)], leaves.at[pl.ds(0, N_GY - 1)]
        return copy(src, dst, near_s.at[0], near_r.at[0], (gx, (gy + 1) % N_GY))

    @pl.loop(1, N_GY)
    def _(k):
        pay_copy((gy + k) % N_GY, gy).start()

    loads[0].wait()
    row = lax.broadcasted_iota(jnp.int32, (16, 128), 0)
    wanted = jnp.full((16, 128), -1, jnp.int32)
    for leaf in range(2):
        for n in range(NEAR):
            wanted = jnp.where(row == leaf * NEAR + n, near[leaf, n], wanted)
    asked[gy] = wanted.astype(F32).astype(BF16)

    @pl.loop(1, N_GY)
    def _(k):
        req_copy((gy + k) % N_GY, gy).start()

    @pl.loop(0, 2)
    def _(leaf):
        at = pl.ds(pl.multiple_of(leaf * LEAF, LEAF), LEAF)
        wide = own_right[leaf].astype(F32)
        both = jnp.concatenate([wide[:D], turned(wide[D:]), jnp.zeros((48, LEAF), F32)], axis=0)
        own_left[leaf] = both.T.astype(BF16)
        own[leaf, 0:D] = points[:, at]
        own[leaf, D:LEAF_ROWS] = residual[:, at].astype(BF16)

    for load in loads[4:]:
        load.wait()

    def tile_term(leaf, right, values):
        tile = jnp.exp2(SCALE * dot(own_left[leaf, :, :AUG], right)).astype(BF16)
        return dot(tile, values, ((1,), (1,)))

    @pl.loop(0, 2)
    def _(leaf):
        near_acc[leaf] = tile_term(leaf, own_right[leaf], own[leaf, D:LEAF_ROWS])

    all_pay().wait_recv()

    def half(row, h):
        return nodes.at[pl.ds(FIRST + row * N_GY + h * 8, 8), pl.ds(0, SENT)]

    def row_of(step, other=False):
        return 2 * ((y + step) % N_Y) + (1 - core if other else core)

    def y_copy(step, h, source):
        to = (row_of(step), gy)
        k = 0 if step == 1 else 1
        return copy(half(gx, h), half(row_of(source), h), y_s.at[k, h], y_r.at[k, h], to)

    def on_copy(step, source):
        h = k = 0 if step == 1 else 1
        return copy(half(row_of(-step), h), half(row_of(source), h), on_s.at[k], on_r.at[k], (row_of(step), gy))

    def sib_copy(h, other):
        return copy(half(row_of(2), h), half(row_of(2, other), h), sib_s.at[h], sib_r.at[h], (sibling, gy))

    for h in range(2):
        y_copy(1, h, 0).start()
        y_copy(-1, 1 - h, 0).start()

    this = (2 * me + 1).astype(F32)
    leaves[gy] = own[0]

    @pl.loop(1, N_GY)
    def _(k):
        peer = (gy + k) % N_GY
        req_copy(peer, peer).wait_recv()
        second = jnp.where(asked[peer].astype(F32) == this, 1.0, 0.0)
        second = jnp.max(second, axis=0, keepdims=True)
        second = jnp.concatenate([second] * 4, axis=1)
        for r in range(0, LEAF_ROWS, 32):
            at = pl.ds(r, 32)
            stage[peer, at] = jnp.where(
                jnp.broadcast_to(second, (32, LEAF)) > 0.5, own[1, at].astype(F32), own[0, at].astype(F32)
            ).astype(BF16)
        near_copy(peer, gy).start()

    def right_of(node):
        return jnp.concatenate([node[:D], node[SENT:]], axis=0)

    def build(first, count):
        done = []
        for i in range(count):
            u = first + i
            a, b = nodes[2 * u + 1], nodes[2 * u + 2]
            choice = jnp.broadcast_to(upper[pl.ds(u, 1), :], (AUG, RANK))
            lane = jnp.bitwise_and(choice, RANK - 1)
            from_a, from_b = (
                jnp.take_along_axis(right_of(x).astype(F32), lane, axis=1, mode="promise_in_bounds") for x in (a, b)
            )
            right = jnp.where(choice < RANK, from_a, from_b)
            left = jnp.concatenate([right[:D], turned(right[D:])], axis=0).astype(BF16)
            both = jnp.concatenate([a, b], axis=1)
            tile = jnp.exp2(SCALE * dot(left, right_of(both), ((0,), (0,)))).astype(BF16)
            sums = dot(both[D:], tile, ((1,), (1,)))
            weights = sums[:NRHS] / sums[NRHS + 4 : NRHS + 5]
            done.append(jnp.concatenate([right[:D], weights, right[D:]], axis=0).astype(BF16))
        for i, node in enumerate(done):
            nodes[first + i] = node

    def build_row(row):
        for h in range(2):
            first = FIRST + row * N_GY + h * 8
            wide = jnp.concatenate([nodes[first + i, 0:D].astype(F32) for i in range(8)], axis=1)
            rows = square_rows(wide).astype(BF16)
            for i in range(8):
                nodes[first + i, SENT:PAY] = rows[:, i * RANK : (i + 1) * RANK]
        build(63 + row * 8, 8)
        build(31 + row * 4, 4)
        build(15 + row * 2, 2)
        build(7 + row, 1)

    def near_tile(n):
        leaf, pair = n // (NEAR // 2), n % (NEAR // 2)
        got = [leaves[(near[leaf, 2 * pair + i] // 2) % N_GY] for i in range(2)]
        got = jnp.concatenate(got, axis=1)
        right = jnp.concatenate([got[:D], square_rows(got[:D].astype(F32)).astype(BF16)], axis=0)
        near_acc[leaf] = near_acc[leaf] + tile_term(leaf, right, got[D:])

    def run(row, level):
        return nodes.at[pl.ds(2**level - 1 + row * (2**level // N_GX), 2**level // N_GX)]

    def full_copy(step, level, other):
        src, dst = run(row_of(step), level), run(row_of(step, other), level)
        return copy(src, dst, full_s.at[0], full_r.at[0], (sibling, gy))

    def all_full():
        part = nodes.at[pl.ds(0, 3 * (2 * N_GY - 1))]
        return copy(part, part, full_s.at[0], full_r.at[0], (sibling, gy))

    @pl.loop(0, N_Y + 1)
    def _(i):
        @pl.when(i == 1)
        def _():
            for step in (1, -1):
                h = 0 if step == 1 else 1
                y_copy(step, h, -step).wait_recv()
                on_copy(step, -step).start()
            y_copy(-1, 0, 1).wait_recv()

        @pl.when(i == 2)
        def _():
            y_copy(1, 1, -1).wait_recv()

        @pl.when(i == 3)
        def _():
            for step in (1, -1):
                on_copy(step, 2).wait_recv()
                sib_copy(0 if step == 1 else 1, False).start()

        @pl.when(i == 4)
        def _():
            for h in range(2):
                sib_copy(h, True).wait_recv()

        turn = i - i // N_Y
        away = turn + turn // 2 - 2 * (turn // 3)
        build_row(2 * ((y + away) % N_Y) + (core + i // N_Y) % 2)

        @pl.when(i < 3)
        def _():
            for level in range(7, 2, -1):
                full_copy(away, level, False).start()

    all_full().wait_recv()

    build(3, 4)
    build(1, 2)
    build(0, 1)

    far_acc[...] = jnp.zeros_like(far_acc)

    @pl.loop(0, FAR // 4)
    def _(n):
        leaf, group = n // (FAR // 8), n % (FAR // 8)
        got = jnp.concatenate([nodes[far[leaf, 8 * group + i]] for i in range(8)], axis=1)
        far_acc[leaf] = far_acc[leaf] + tile_term(leaf, right_of(got), got[D:SENT])

    all_near().wait_recv()

    pl.loop(0, NEAR)(near_tile)

    for leaf in range(2):
        at = pl.ds(leaf * LEAF, LEAF)
        terms = near_acc[leaf] * (1.0 / math.sqrt(LEAF)) + far_acc[leaf] * (1.0 / RANK)
        image[:, at] = residual[:, at] + terms.T

    both = jnp.concatenate([image[...], residual[...]], axis=0)
    gram = dot(image[...], both, ((1,), (1,)), FULL)
    part1[gy] = jnp.concatenate([gram[:16], gram[16:]], axis=1)

    def one_copy(peer, slot):
        return copy(part1.at[gy], part1.at[slot], one_s.at[0], one_r.at[0], (gx, peer))

    def all_one():
        part = part1.at[pl.ds(0, N_GY - 1)]
        return copy(part, part, one_s.at[0], one_r.at[0], (gx, (gy + 1) % N_GY))

    def all_two():
        part = part2.at[pl.ds(0, N_GX - 1)]
        return copy(part, part, two_s.at[0], two_r.at[0], ((gx + 1) % N_GX, gy))

    def two_copy(peer, slot):
        return copy(part2.at[gx], part2.at[slot], two_s.at[0], two_r.at[0], (peer, gy))

    @pl.loop(1, N_GY)
    def _(k):
        one_copy((gy + k) % N_GY, gy).start()

    @pl.loop(1, N_GY)
    def _(k):
        peer = (gy + k) % N_GY
        req_copy(peer, gy).wait_send()

    all_pay().wait_send()
    all_near().wait_send()
    for step in (1, -1):
        for h in range(2):
            y_copy(step, h, 0).wait_send()
        on_copy(step, -step).wait_send()
    for h in range(2):
        sib_copy(h, False).wait_send()

    all_full().wait_send()

    all_one().wait_recv()

    total = part1[0]
    for k in range(1, N_GY):
        total += part1[k]
    part2[gx] = total

    @pl.loop(1, N_GX)
    def _(k):
        two_copy((gx + k) % N_GX, gx).start()

    all_one().wait_send()

    all_two().wait_recv()

    total = part2[0]
    for k in range(1, N_GX):
        total += part2[k]

    work = jnp.concatenate([total, pltpu.roll(total, 64, 1)], axis=0)

    def eight(_, work):
        columns = [jnp.broadcast_to(work[:, i : i + 1], (NRHS, 128)) for i in range(8)]
        block = [[columns[j][i : i + 1] for j in range(8)] for i in range(8)]
        rows = [work[i : i + 1] for i in range(8)]
        for i in range(8):
            inverse = 1.0 / block[i][i]
            rows[i] = rows[i] * inverse
            for j in range(i + 1, 8):
                block[i][j] = block[i][j] * inverse
            for r in range(i + 1, 8):
                for j in range(i + 1, 8):
                    block[r][j] = block[r][j] - block[r][i] * block[i][j]
                rows[r] = rows[r] - block[r][i] * rows[i]
        for i in range(7, 0, -1):
            for r in range(i):
                rows[r] = rows[r] - block[r][i] * rows[i]
        rest = work
        for i in range(8):
            rest = rest - columns[i] * rows[i]
        return pltpu.roll(jnp.concatenate([rest[8:], *rows], axis=0), 120, 1)

    work = lax.fori_loop(0, NRHS // 8, eight, work)
    coeffs[...] = work

    all_two().wait_send()


def update_body(work, solution, residual, image, solution_next, residual_next, image_out):
    step = work[:, :NRHS].T
    solution_next[...] = solution[...] + dot(step, residual[...], precision=FULL)
    residual_next[...] = residual[...] - dot(step, image[...], precision=FULL)
    image_out[...] = image[...]


def shards(points, solution, residual, near_leaves, node_skeleton, upper_skeleton, far_nodes):
    vmem, hbm = (pl.BlockSpec(memory_space=m) for m in (pltpu.VMEM, pltpu.HBM))
    dma = pltpu.SemaphoreType.DMA
    residual_t = residual.T
    image_t, work = pl.pallas_call(
        kernel_body,
        out_shape=(
            jax.ShapeDtypeStruct((NRHS, CPD), F32),
            jax.ShapeDtypeStruct((NRHS, 128), F32),
        ),
        in_specs=[hbm] * 6,
        out_specs=(vmem, vmem),
        scratch_shapes=[
            pltpu.VMEM((D, CPD), BF16),
            pltpu.VMEM((NRHS, CPD), F32),
            pltpu.SMEM((2, NEAR), jnp.int32),
            pltpu.VMEM((1, RANK), jnp.int32),
            pltpu.VMEM((FIRST, RANK), jnp.int32),
            pltpu.SMEM((2, FAR), jnp.int32),
            pltpu.VMEM((NODES, PAY, RANK), BF16),
            pltpu.VMEM((2, LEAF_ROWS, LEAF), BF16),
            pltpu.VMEM((2, AUG, LEAF), BF16),
            pltpu.VMEM((2, LEAF, 128), BF16),
            pltpu.VMEM((N_GY, 16, 128), BF16),
            pltpu.VMEM((N_GY, LEAF_ROWS, LEAF), BF16),
            pltpu.VMEM((N_GY, LEAF_ROWS, LEAF), BF16),
            pltpu.VMEM((2, LEAF, NRHS), F32),
            pltpu.VMEM((2, LEAF, NRHS), F32),
            pltpu.VMEM((N_GY, 16, 128), F32),
            pltpu.VMEM((N_GX, 16, 128), F32),
            dma((6,)),
            dma((N_GY,)), dma((N_GY,)), dma((1,)), dma((1,)), dma((1,)), dma((1,)),
            dma((2, 2)), dma((2, 2)), dma((2,)), dma((2,)), dma((2,)), dma((2,)), dma((1,)), dma((1,)),
            dma((1,)), dma((1,)), dma((1,)), dma((1,)),
        ],
        compiler_params=pltpu.CompilerParams(
            collective_id=0, has_side_effects=True, vmem_limit_bytes=60 * 2**20
        ),
    )(points.T, residual_t, near_leaves, node_skeleton, upper_skeleton, far_nodes)
    outs = pl.pallas_call(
        update_body,
        out_shape=(jax.ShapeDtypeStruct((NRHS, CPD), F32),) * 3,
        in_specs=[vmem] * 4,
        out_specs=(vmem,) * 3,
    )(work, solution.T, residual_t, image_t)
    return tuple(o.T for o in outs)


def solution(mesh):
    split = P(("gx", "gy"), None)
    return jax.shard_map(
        shards,
        mesh=mesh,
        in_specs=(split, split, split, split, split, P(), split),
        out_specs=(split, split, split),
        check_vma=False,
    )
```

```python
import math

import jax
import jax.numpy as jnp
from jax import lax
from jax.experimental import pallas as pl
from jax.experimental.pallas import tpu as pltpu
from jax.sharding import PartitionSpec as P

D = 64
NRHS = 32
LEAF = 512
RANK = 128
NEAR = 4
FAR = 16
CPD = 1024
N_GX = 8
N_GY = 16
N_Y = 4
NODES = 255
FIRST = 127
AUG = D + 16
SENT = D + NRHS
PAY = SENT + 16
LEAF_ROWS = D + NRHS
SCALE = math.log2(math.e) / D
FULL = lax.Precision.HIGHEST
F32, BF16 = jnp.float32, jnp.bfloat16
MESH = pl.DeviceIdType.MESH


def dot(a, b, contract=((1,), (0,)), precision=None):
    return lax.dot_general(a, b, (contract, ((), ())), precision=precision, preferred_element_type=F32)


def square_rows(wide):
    half = -0.5 * jnp.sum(wide * wide, axis=0, keepdims=True)
    high = half.astype(BF16).astype(F32)
    rest = half - high
    middle = rest.astype(BF16).astype(F32)
    low = rest - middle
    row = lax.broadcasted_iota(jnp.int32, (16, wide.shape[1]), 0)
    ones = jnp.where((row >= 4) & (row < 7), 1.0, 0.0)
    return jnp.where(row == 0, high, jnp.where(row == 1, middle, jnp.where(row == 2, low, ones)))


def turned(rows):
    return jnp.concatenate([pltpu.roll(rows[:8], 4, 0), rows[8:]], axis=0)


def kernel_body(
    points_in, residual_in, near_in, skeleton_in, upper_in, far_in,
    image, coeffs,
    points, residual, near, skeleton, upper, far,
    nodes, own, own_right, own_left, asked, stage, leaves, near_acc, far_acc, part1, part2,
    in_s, req_s, req_r, pay_s, pay_r, near_s, near_r, y_s, y_r, on_s, on_r, sib_s, sib_r, full_s, full_r,
    one_s, one_r, two_s, two_r,
):
    gx, gy = lax.axis_index("gx"), lax.axis_index("gy")
    y, core = gx // 2, gx % 2
    me = gx * N_GY + gy
    sibling = 2 * y + (1 - core)

    pairs = ((near_in, near), (skeleton_in, skeleton), (points_in, points), (residual_in, residual), (upper_in, upper), (far_in, far))
    loads = [pltpu.make_async_copy(a, b, in_s.at[i]) for i, (a, b) in enumerate(pairs)]
    for load in loads:
        load.start()

    barrier = pltpu.get_barrier_semaphore()

    @pl.loop(1, N_GY)
    def _(k):
        pl.semaphore_signal(barrier, inc=1, device_id=(gx, (gy + k) % N_GY), device_id_type=MESH)

    @pl.loop(1, N_GX)
    def _(k):
        pl.semaphore_signal(barrier, inc=1, device_id=((gx + k) % N_GX, gy), device_id_type=MESH)

    def copy(src, dst, send, recv, device):
        return pltpu.make_async_remote_copy(
            src_ref=src, dst_ref=dst, send_sem=send, recv_sem=recv, device_id=device, device_id_type=MESH
        )

    for load in loads[1:4]:
        load.wait()

    @pl.loop(0, 2)
    def _(leaf):
        at = pl.ds(pl.multiple_of(leaf * LEAF, LEAF), LEAF)
        own_right[leaf, 0:D] = points[:, at]
        own_right[leaf, D:AUG] = square_rows(points[:, at].astype(F32)).astype(BF16)

    place = lax.broadcasted_iota(jnp.int32, (CPD, RANK), 0)
    skel = dot(points[...], jnp.where(place == skeleton[...], 1.0, 0.0).astype(BF16))
    rows = square_rows(skel)
    left = jnp.concatenate([skel, turned(rows), jnp.zeros((48, RANK), F32)], axis=0).T.astype(BF16)
    weights = jnp.zeros((NRHS, RANK), F32)
    for leaf in range(2):
        tile = jnp.exp2(SCALE * dot(left[:, :AUG], own_right[leaf]))
        weights += dot(residual[:, pl.ds(leaf * LEAF, LEAF)], tile, ((1,), (1,)), FULL)
    mine = FIRST + me
    nodes[mine, 0:D] = skel.astype(BF16)
    nodes[mine, D:SENT] = (weights * (1.0 / math.sqrt(CPD))).astype(BF16)

    far_acc[...] = jnp.zeros_like(far_acc)
    pl.semaphore_wait(barrier, N_GY - 1 + N_GX - 1)

    def req_copy(peer, slot):
        return copy(asked.at[gy], asked.at[slot], req_s.at[peer], req_r.at[slot], (gx, peer))

    def pay_copy(peer, slot):
        at = FIRST + gx * N_GY + slot
        return copy(nodes.at[mine, pl.ds(0, SENT)], nodes.at[at, pl.ds(0, SENT)], pay_s.at[0], pay_r.at[0], (gx, peer))

    def all_pay():
        part = nodes.at[pl.ds(FIRST + gx * N_GY, N_GY - 1), pl.ds(0, SENT)]
        return copy(part, part, pay_s.at[0], pay_r.at[0], (gx, (gy + 1) % N_GY))

    def near_copy(peer, slot):
        return copy(stage.at[peer], leaves.at[slot], near_s.at[0], near_r.at[0], (gx, peer))

    def all_near():
        src, dst = stage.at[pl.ds(0, N_GY - 1)], leaves.at[pl.ds(0, N_GY - 1)]
        return copy(src, dst, near_s.at[0], near_r.at[0], (gx, (gy + 1) % N_GY))

    @pl.loop(1, N_GY)
    def _(k):
        pay_copy((gy + k) % N_GY, gy).start()

    loads[0].wait()
    row = lax.broadcasted_iota(jnp.int32, (16, 128), 0)
    wanted = jnp.full((16, 128), -1, jnp.int32)
    for leaf in range(2):
        for n in range(NEAR):
            wanted = jnp.where(row == leaf * NEAR + n, near[leaf, n], wanted)
    asked[gy] = wanted.astype(F32).astype(BF16)

    @pl.loop(1, N_GY)
    def _(k):
        req_copy((gy + k) % N_GY, gy).start()

    @pl.loop(0, 2)
    def _(leaf):
        at = pl.ds(pl.multiple_of(leaf * LEAF, LEAF), LEAF)
        wide = own_right[leaf].astype(F32)
        both = jnp.concatenate([wide[:D], turned(wide[D:]), jnp.zeros((48, LEAF), F32)], axis=0)
        own_left[leaf] = both.T.astype(BF16)
        own[leaf, 0:D] = points[:, at]
        own[leaf, D:LEAF_ROWS] = residual[:, at].astype(BF16)

    for load in loads[4:]:
        load.wait()

    def tile_term(leaf, right, values):
        tile = jnp.exp2(SCALE * dot(own_left[leaf, :, :AUG], right)).astype(BF16)
        return dot(tile, values, ((1,), (1,)))

    @pl.loop(0, 2)
    def _(leaf):
        near_acc[leaf] = tile_term(leaf, own_right[leaf], own[leaf, D:LEAF_ROWS])

    all_pay().wait_recv()

    def half(row, h):
        return nodes.at[pl.ds(FIRST + row * N_GY + h * 8, 8), pl.ds(0, SENT)]

    def row_of(step, other=False):
        return 2 * ((y + step) % N_Y) + (1 - core if other else core)

    def y_copy(step, h, source):
        to = (row_of(step), gy)
        k = 0 if step == 1 else 1
        return copy(half(gx, h), half(row_of(source), h), y_s.at[k, h], y_r.at[k, h], to)

    def on_copy(step, source):
        h = k = 0 if step == 1 else 1
        return copy(half(row_of(-step), h), half(row_of(source), h), on_s.at[k], on_r.at[k], (row_of(step), gy))

    def sib_copy(h, other):
        return copy(half(row_of(2), h), half(row_of(2, other), h), sib_s.at[h], sib_r.at[h], (sibling, gy))

    for h in range(2):
        y_copy(1, h, 0).start()
        y_copy(-1, 1 - h, 0).start()

    this = (2 * me + 1).astype(F32)
    leaves[gy] = own[0]

    @pl.loop(1, N_GY)
    def _(k):
        peer = (gy + k) % N_GY
        req_copy(peer, peer).wait_recv()
        second = jnp.where(asked[peer].astype(F32) == this, 1.0, 0.0)
        second = jnp.max(second, axis=0, keepdims=True)
        second = jnp.concatenate([second] * 4, axis=1)
        for r in range(0, LEAF_ROWS, 32):
            at = pl.ds(r, 32)
            stage[peer, at] = jnp.where(
                jnp.broadcast_to(second, (32, LEAF)) > 0.5, own[1, at].astype(F32), own[0, at].astype(F32)
            ).astype(BF16)
        near_copy(peer, gy).start()

    def right_of(node):
        return jnp.concatenate([node[:D], node[SENT:]], axis=0)

    def build(first, count):
        done = []
        for i in range(count):
            u = first + i
            a, b = nodes[2 * u + 1], nodes[2 * u + 2]
            choice = jnp.broadcast_to(upper[pl.ds(u, 1), :], (AUG, RANK))
            lane = jnp.bitwise_and(choice, RANK - 1)
            from_a, from_b = (
                jnp.take_along_axis(right_of(x).astype(F32), lane, axis=1, mode="promise_in_bounds") for x in (a, b)
            )
            right = jnp.where(choice < RANK, from_a, from_b)
            left = jnp.concatenate([right[:D], turned(right[D:])], axis=0).astype(BF16)
            both = jnp.concatenate([a, b], axis=1)
            tile = jnp.exp2(SCALE * dot(left, right_of(both), ((0,), (0,)))).astype(BF16)
            sums = dot(both[D:], tile, ((1,), (1,)))
            weights = sums[:NRHS] / sums[NRHS + 4 : NRHS + 5]
            done.append(jnp.concatenate([right[:D], weights, right[D:]], axis=0).astype(BF16))
        for i, node in enumerate(done):
            nodes[first + i] = node

    def build_row(row):
        for h in range(2):
            first = FIRST + row * N_GY + h * 8
            wide = jnp.concatenate([nodes[first + i, 0:D].astype(F32) for i in range(8)], axis=1)
            rows = square_rows(wide).astype(BF16)
            for i in range(8):
                nodes[first + i, SENT:PAY] = rows[:, i * RANK : (i + 1) * RANK]
        build(63 + row * 8, 8)
        build(31 + row * 4, 4)
        build(15 + row * 2, 2)
        build(7 + row, 1)

    def near_tile(n):
        leaf, pair = n // (NEAR // 2), n % (NEAR // 2)
        got = [leaves[(near[leaf, 2 * pair + i] // 2) % N_GY] for i in range(2)]
        got = jnp.concatenate(got, axis=1)
        right = jnp.concatenate([got[:D], square_rows(got[:D].astype(F32)).astype(BF16)], axis=0)
        near_acc[leaf] = near_acc[leaf] + tile_term(leaf, right, got[D:])

    def run(row, level):
        return nodes.at[pl.ds(2**level - 1 + row * (2**level // N_GX), 2**level // N_GX)]

    def full_copy(step, level, other):
        src, dst = run(row_of(step), level), run(row_of(step, other), level)
        return copy(src, dst, full_s.at[0], full_r.at[0], (sibling, gy))

    def all_full():
        part = nodes.at[pl.ds(0, 3 * (2 * N_GY - 1))]
        return copy(part, part, full_s.at[0], full_r.at[0], (sibling, gy))

    @pl.loop(0, N_Y + 1)
    def _(i):
        @pl.when(i == 1)
        def _():
            for step in (1, -1):
                h = 0 if step == 1 else 1
                y_copy(step, h, -step).wait_recv()
                on_copy(step, -step).start()
            y_copy(-1, 0, 1).wait_recv()

        @pl.when(i == 2)
        def _():
            y_copy(1, 1, -1).wait_recv()

        @pl.when(i == 3)
        def _():
            for step in (1, -1):
                on_copy(step, 2).wait_recv()
                sib_copy(0 if step == 1 else 1, False).start()

        @pl.when(i == 4)
        def _():
            for h in range(2):
                sib_copy(h, True).wait_recv()

        turn = i - i // N_Y
        away = turn + turn // 2 - 2 * (turn // 3)
        build_row(2 * ((y + away) % N_Y) + (core + i // N_Y) % 2)

        @pl.when(i < 3)
        def _():
            for level in range(7, 2, -1):
                full_copy(away, level, False).start()

    all_full().wait_recv()

    build(3, 4)
    build(1, 2)
    build(0, 1)

    @pl.loop(0, FAR // 4)
    def _(n):
        leaf, group = n // (FAR // 8), n % (FAR // 8)
        got = jnp.concatenate([nodes[far[leaf, 8 * group + i]] for i in range(8)], axis=1)
        far_acc[leaf] = far_acc[leaf] + tile_term(leaf, right_of(got), got[D:SENT])

    all_near().wait_recv()

    pl.loop(0, NEAR)(near_tile)

    for leaf in range(2):
        at = pl.ds(leaf * LEAF, LEAF)
        terms = near_acc[leaf] * (1.0 / math.sqrt(LEAF)) + far_acc[leaf] * (1.0 / RANK)
        image[:, at] = residual[:, at] + terms.T

    both = jnp.concatenate([image[...], residual[...]], axis=0)
    gram = dot(image[...], both, ((1,), (1,)), FULL)
    part1[gy] = jnp.concatenate([gram[:16], gram[16:]], axis=1)

    def one_copy(peer, slot):
        return copy(part1.at[gy], part1.at[slot], one_s.at[0], one_r.at[0], (gx, peer))

    def all_one():
        part = part1.at[pl.ds(0, N_GY - 1)]
        return copy(part, part, one_s.at[0], one_r.at[0], (gx, (gy + 1) % N_GY))

    def all_two():
        part = part2.at[pl.ds(0, N_GX - 1)]
        return copy(part, part, two_s.at[0], two_r.at[0], ((gx + 1) % N_GX, gy))

    def two_copy(peer, slot):
        return copy(part2.at[gx], part2.at[slot], two_s.at[0], two_r.at[0], (peer, gy))

    @pl.loop(1, N_GY)
    def _(k):
        one_copy((gy + k) % N_GY, gy).start()

    @pl.loop(1, N_GY)
    def _(k):
        peer = (gy + k) % N_GY
        req_copy(peer, gy).wait_send()

    all_pay().wait_send()
    all_near().wait_send()
    for step in (1, -1):
        for h in range(2):
            y_copy(step, h, 0).wait_send()
        on_copy(step, -step).wait_send()
    for h in range(2):
        sib_copy(h, False).wait_send()

    all_full().wait_send()

    all_one().wait_recv()

    total = part1[0]
    for k in range(1, N_GY):
        total += part1[k]
    part2[gx] = total

    @pl.loop(1, N_GX)
    def _(k):
        two_copy((gx + k) % N_GX, gx).start()

    all_one().wait_send()

    all_two().wait_recv()

    total = part2[0]
    for k in range(1, N_GX):
        total += part2[k]

    work = jnp.concatenate([total, pltpu.roll(total, 64, 1)], axis=0)

    def eight(_, work):
        columns = [jnp.broadcast_to(work[:, i : i + 1], (NRHS, 128)) for i in range(8)]
        block = [[columns[j][i : i + 1] for j in range(8)] for i in range(8)]
        rows = [work[i : i + 1] for i in range(8)]
        for i in range(8):
            inverse = 1.0 / block[i][i]
            rows[i] = rows[i] * inverse
            for j in range(i + 1, 8):
                block[i][j] = block[i][j] * inverse
            for r in range(i + 1, 8):
                for j in range(i + 1, 8):
                    block[r][j] = block[r][j] - block[r][i] * block[i][j]
                rows[r] = rows[r] - block[r][i] * rows[i]
        for i in range(7, 0, -1):
            for r in range(i):
                rows[r] = rows[r] - block[r][i] * rows[i]
        rest = work
        for i in range(8):
            rest = rest - columns[i] * rows[i]
        return pltpu.roll(jnp.concatenate([rest[8:], *rows], axis=0), 120, 1)

    work = lax.fori_loop(0, NRHS // 8, eight, work)
    coeffs[...] = work

    all_two().wait_send()


def update_body(work, solution, residual, image, solution_next, residual_next, image_out):
    step = work[:, :NRHS].T
    solution_next[...] = solution[...] + dot(step, residual[...], precision=FULL)
    residual_next[...] = residual[...] - dot(step, image[...], precision=FULL)
    image_out[...] = image[...]


def shards(points, solution, residual, near_leaves, node_skeleton, upper_skeleton, far_nodes):
    vmem, hbm = (pl.BlockSpec(memory_space=m) for m in (pltpu.VMEM, pltpu.HBM))
    dma = pltpu.SemaphoreType.DMA
    residual_t = residual.T
    image_t, work = pl.pallas_call(
        kernel_body,
        out_shape=(
            jax.ShapeDtypeStruct((NRHS, CPD), F32),
            jax.ShapeDtypeStruct((NRHS, 128), F32),
        ),
        in_specs=[hbm] * 6,
        out_specs=(vmem, vmem),
        scratch_shapes=[
            pltpu.VMEM((D, CPD), BF16),
            pltpu.VMEM((NRHS, CPD), F32),
            pltpu.SMEM((2, NEAR), jnp.int32),
            pltpu.VMEM((1, RANK), jnp.int32),
            pltpu.VMEM((FIRST, RANK), jnp.int32),
            pltpu.SMEM((2, FAR), jnp.int32),
            pltpu.VMEM((NODES, PAY, RANK), BF16),
            pltpu.VMEM((2, LEAF_ROWS, LEAF), BF16),
            pltpu.VMEM((2, AUG, LEAF), BF16),
            pltpu.VMEM((2, LEAF, 128), BF16),
            pltpu.VMEM((N_GY, 16, 128), BF16),
            pltpu.VMEM((N_GY, LEAF_ROWS, LEAF), BF16),
            pltpu.VMEM((N_GY, LEAF_ROWS, LEAF), BF16),
            pltpu.VMEM((2, LEAF, NRHS), F32),
            pltpu.VMEM((2, LEAF, NRHS), F32),
            pltpu.VMEM((N_GY, 16, 128), F32),
            pltpu.VMEM((N_GX, 16, 128), F32),
            dma((6,)),
            dma((N_GY,)), dma((N_GY,)), dma((1,)), dma((1,)), dma((1,)), dma((1,)),
            dma((2, 2)), dma((2, 2)), dma((2,)), dma((2,)), dma((2,)), dma((2,)), dma((1,)), dma((1,)),
            dma((1,)), dma((1,)), dma((1,)), dma((1,)),
        ],
        compiler_params=pltpu.CompilerParams(
            collective_id=0, has_side_effects=True, vmem_limit_bytes=60 * 2**20
        ),
    )(points.T, residual_t, near_leaves, node_skeleton, upper_skeleton, far_nodes)
    outs = pl.pallas_call(
        update_body,
        out_shape=(jax.ShapeDtypeStruct((NRHS, CPD), F32),) * 3,
        in_specs=[vmem] * 4,
        out_specs=(vmem,) * 3,
    )(work, solution.T, residual_t, image_t)
    return tuple(o.T for o in outs)


def solution(mesh):
    split = P(("gx", "gy"), None)
    return jax.shard_map(
        shards,
        mesh=mesh,
        in_specs=(split, split, split, split, split, P(), split),
        out_specs=(split, split, split),
        check_vma=False,
    )
```
